512 devices in a mesh: dp: 64 (over z, y), seq: 8 (over x, core).
Axes of the slice: x: 4, y: 4, z: 16, core: 2. Of those that a mesh axis runs over, the one named last changes fastest.
Arguments:
- queries: bfloat16 [98304, 4096], P(('dp', 'seq')), may hold values from -10 to 10
- key_value: bfloat16 [98304, 8, 2, 128], P(('dp', 'seq')), may hold values from -10 to 10
- route_group: int32 [98304], P(('dp', 'seq')), may hold values from 0 to 63, as said below
- arrive_slot: int32 [98304], P(('dp', 'seq')), may hold values from 0 to 383, as said below
- segment_ids: int32 [64, 1536], P('dp', 'seq'), may hold values from 0 to 7, never falling along the last dimension, each value on 1 to 384 neighbouring positions
Outputs:
- attended: bfloat16 [98304, 4096], P(('dp', 'seq'))
The draws below stay inside these ranges and needn't reach their ends.
Inputs may be any that keep to these rules, and one draw needn't show every extreme that they name: Rows keep their index along seq: the row of device (g, s) goes to device (route_group, s). Each device sends 6 rows to one group, 3 rows to most others and none to one; every device receives 192 rows. For one index s along seq, how many rows device g sends to group (g + k) modulo the number of groups depends on k only. `arrive_slot`: equals src * 6 + r, where src is the sending group and r the place of the row among that group's rows sent to this device, in row order; with route_group it maps rows one to one.
All inputs are finite; a program needn't handle non-finite values.
Results may differ from the reference program's by a relative error of at most 0.0046.
Values may be sent and summed in bfloat16 or wider, within the bound.
No kernel may reach another device: no remote copies, remote signals or barrier semaphores. Data moves between devices by JAX's collectives and lax.ppermute only.
A program may use at most 64 MiB of HBM per device.

```python
import math
import jax
import jax.numpy as jnp
import numpy as np
from jax import lax

QH = 32
KVH = 8
HD = 128
TOK_DEV = 192
PROOFS = 8
SEQ_LEN = 1536
LONGEST = 384
CAP = 6
TOKENS = 98304
N_DP = 64
N_SEQ = 8


def packing(key):
    per_round = TOK_DEV // N_DP
    key_shift, key_place = jax.random.split(key)
    shifts = jax.vmap(lambda item: jax.random.permutation(item, N_DP))(jax.random.split(key_shift, N_SEQ)).astype(jnp.int32)
    shifts = shifts.at[:, 1].set(shifts[:, 0])
    rounds = jnp.arange(TOK_DEV, dtype=jnp.int32) // per_round
    groups = jnp.arange(N_DP, dtype=jnp.int32)
    routed = (groups[:, None, None] + shifts[None, :, :][:, :, rounds]) % N_DP
    blocks = jax.vmap(lambda item: jax.random.permutation(item, N_DP))(jax.random.split(key_place, N_DP * N_SEQ)).astype(jnp.int32)
    blocks = blocks.reshape(N_DP, N_SEQ, N_DP)
    places = jnp.arange(TOK_DEV, dtype=jnp.int32)
    arrival_round = blocks[:, :, places // per_round]
    offset = places % per_round
    seq_ids = jnp.arange(N_SEQ, dtype=jnp.int32)[None, :, None]
    sender = (groups[:, None, None] - shifts[seq_ids, arrival_round]) % N_DP
    order_rank = (arrival_round == 1).astype(jnp.int32) * per_round + offset[None, None, :]
    arrive = sender * CAP + order_rank
    return (routed.reshape(TOKENS).astype(jnp.int32), arrive.reshape(TOKENS).astype(jnp.int32))


def draw_route_group(key, part):
    routed, arrive = packing(key)
    return routed


def draw_arrive_slot(key, part):
    routed, arrive = packing(key)
    return arrive


def draw_queries(key, part):
    key = jax.random.fold_in(key, 11)
    values = jnp.clip(jax.random.normal(key, (TOKENS, QH * HD), jnp.float32), -6.0, 6.0)
    return values.astype(jnp.bfloat16)


def draw_key_value(key, part):
    key = jax.random.fold_in(key, 12)
    values = jnp.clip(jax.random.normal(key, (TOKENS, KVH, 2, HD), jnp.float32), -6.0, 6.0)
    return values.astype(jnp.bfloat16)


def length_profile(amount, total, most, skew):
    portions = [(1 << 20) // math.isqrt(standing ** skew) + 1 for standing in range(2, amount + 1)]
    rest, given = total - most - (amount - 1), [1] * (amount - 1)
    while rest > 0:
        free = [i for i in range(amount - 1) if given[i] < most]
        mass, budget = sum([portions[i] for i in free]), rest
        for i in free:
            addition = min(most - given[i], max(1, budget * portions[i] // mass), rest)
            given[i] = given[i] + addition
            rest = rest - addition
    return np.array([most] + given)


def uneven_parts(stream_key, amount, total, limit, skew):
    if amount == 2:
        one = jax.random.randint(stream_key, (), max(1, total - limit), min(limit, total - 1) + 1)
        return jnp.stack([one, total - one])
    sizes = jnp.asarray(length_profile(amount, total, limit, skew), jnp.int32)
    couples = (amount - 1) // 2
    donor, taker = sizes[1:1 + 2 * couples:2], sizes[2:2 + 2 * couples:2]
    margin = jnp.minimum(donor - 1, limit - taker)
    shifted = jax.random.randint(jax.random.fold_in(stream_key, 1), (couples,), 0, 1 << 20) % (margin + 1)
    sizes = sizes.at[1:1 + 2 * couples:2].set(donor - shifted).at[2:2 + 2 * couples:2].set(taker + shifted)
    return sizes[jax.random.permutation(jax.random.fold_in(stream_key, 2), amount)]


def setup_inputs(seed: int = 0) -> dict:
    arg_keys = jax.random.split(jax.random.key(seed), 6)
    queries = draw_queries(jax.random.fold_in(arg_keys[5], 71), 0)
    key_value = draw_key_value(jax.random.fold_in(arg_keys[5], 71), 0)
    route_group = draw_route_group(jax.random.fold_in(arg_keys[5], 71), 0)
    arrive_slot = draw_arrive_slot(jax.random.fold_in(arg_keys[5], 71), 0)
    segment_ids = jax.vmap(lambda own: jnp.searchsorted(jnp.cumsum(uneven_parts(own, PROOFS, SEQ_LEN, LONGEST, 2)), jnp.arange(SEQ_LEN), side="right"))(jax.random.split(arg_keys[4], N_DP)).reshape((N_DP, SEQ_LEN)).astype(jnp.int32)
    return {"queries": queries, "key_value": key_value, "route_group": route_group, "arrive_slot": arrive_slot, "segment_ids": segment_ids}


def attend(queries, key_value, segment):
    total_len = key_value.shape[0]
    kv_heads = key_value.shape[1]
    head_dim = key_value.shape[3]
    grouped = queries.shape[1] // (kv_heads * head_dim)
    scaling = head_dim ** -0.5
    longest = total_len // 4
    block_rows = min(512, total_len)
    blocks = total_len // block_rows
    width = longest + block_rows
    shaped = queries.reshape(total_len, kv_heads, grouped, head_dim)
    padded_kv = jnp.concatenate([jnp.zeros((longest, kv_heads, 2, head_dim), key_value.dtype), key_value], axis=0)
    padded_seg = jnp.concatenate([jnp.full((longest,), -1, jnp.int32), segment.astype(jnp.int32)], axis=0)

    def per_head(head_idx):
        q_head = lax.dynamic_index_in_dim(shaped, head_idx, 1, False).astype(jnp.float32)
        kv_head = lax.dynamic_index_in_dim(padded_kv, head_idx, 1, False).astype(jnp.float32)

        def per_block(block_idx):
            first = (block_idx * block_rows).astype(jnp.int32)
            q_block = lax.dynamic_slice_in_dim(q_head, first, block_rows, 0)
            window = lax.dynamic_slice_in_dim(kv_head, first, width, 0)
            seg_win = lax.dynamic_slice_in_dim(padded_seg, first, width, 0)
            q_seg = lax.dynamic_slice_in_dim(segment.astype(jnp.int32), first, block_rows, 0)
            q_pos = first + jnp.arange(block_rows, dtype=jnp.int32)
            k_pos = first - longest + jnp.arange(width, dtype=jnp.int32)
            visible = (q_pos[:, None] >= k_pos[None, :]) & (q_seg[:, None] == seg_win[None, :])
            scores = jnp.einsum("qgd,sd->gqs", q_block, window[:, 0]) * scaling
            scores = jnp.where(visible[None], scores, -jnp.inf)
            top_score = jnp.max(scores, axis=2, keepdims=True)
            powers = jnp.exp(scores - top_score)
            weights = (powers / jnp.sum(powers, axis=2, keepdims=True)).astype(jnp.bfloat16)
            return jnp.einsum("gqs,sd->qgd", weights.astype(jnp.float32), window[:, 1])

        return lax.map(per_block, jnp.arange(blocks, dtype=jnp.int32))

    outs = lax.map(per_head, jnp.arange(kv_heads, dtype=jnp.int32))
    return outs.transpose(1, 2, 0, 3, 4).reshape(total_len, -1).astype(jnp.bfloat16)


def reference(queries, key_value, route_group, arrive_slot, segment_ids):
    lane_ids = jnp.arange(N_DP, dtype=jnp.int32)
    routed = route_group.reshape(N_DP, N_SEQ, TOK_DEV)
    onehot = (routed[..., None] == lane_ids).astype(jnp.int32)
    before = jnp.cumsum(onehot, axis=2) - onehot
    order_rank = jnp.sum(before * onehot, axis=3).astype(jnp.int32)
    group_ids = jnp.broadcast_to(lane_ids[:, None, None], routed.shape)
    seq_ids = jnp.broadcast_to(jnp.arange(N_SEQ, dtype=jnp.int32)[None, :, None], routed.shape)
    anchor = jnp.arange(TOKENS, dtype=jnp.int32).reshape(routed.shape)
    table = jnp.zeros((N_SEQ, N_DP, N_DP * CAP), jnp.int32)
    table = table.at[seq_ids, routed, group_ids * CAP + order_rank].set(anchor)
    arrived = arrive_slot.reshape(N_DP, N_SEQ, TOK_DEV)
    source = table[seq_ids, group_ids, arrived].reshape(N_DP, SEQ_LEN)

    def per_group(items):
        picks, segment = items
        return attend(queries[picks], key_value[picks], segment)

    outs = lax.map(per_group, (source, segment_ids))
    return outs.reshape(TOKENS, QH * HD)
```

```python
import functools

import jax
import jax.numpy as jnp
from jax import lax
from jax.experimental import pallas as pl
from jax.experimental.pallas import tpu as pltpu
from jax.sharding import Mesh, PartitionSpec as P

ROWS = 192
NZ, NY, NS = 16, 4, 8
PER = 3
TILE = 16
HD = 128
EXT = 9
BF = jnp.bfloat16
VMEM_LIMIT = 48 * 1024 * 1024

VM = pl.BlockSpec(memory_space=pltpu.VMEM)
SM = pl.BlockSpec(memory_space=pltpu.SMEM)
ANY = pl.BlockSpec(memory_space=pl.ANY)


def params(**kw):
    return pltpu.CompilerParams(vmem_limit_bytes=VMEM_LIMIT, **kw)


def pack_kv_kernel(me_ref, rg_ref, kv_ref, q_ref, out_ref, slot_ref, meta_ref, cnt, xrow, qs, sem):
    y = me_ref[0]
    out_ref[...] = jnp.zeros_like(out_ref)
    for i in range(NZ * NY):
        cnt[i] = 0
    for e in range(4):
        xrow[e] = 0
    for e in range(8):
        meta_ref[e] = 0

    def step(i, carry):
        d = rg_ref[i]
        r = cnt[d]
        cnt[d] = r + 1
        over = r >= PER
        gy, gz = d & (NY - 1), d >> 2
        tile = jnp.where(over, NZ * PER + (r - PER) * 3, gz * PER + r)
        out_ref[gy, tile] = kv_ref[i]
        slot_ref[i] = jnp.where(over, ROWS + r - PER, (((gy - y) & (NY - 1)) * NZ + gz) * PER + r)

        @pl.when(over)
        def _():
            xrow[r - PER] = i
            meta_ref[0] = d

        return carry

    lax.fori_loop(0, ROWS, step, 0, unroll=8)
    copies = []
    for e in range(3):
        first = pl.multiple_of((xrow[e] >> 4) << 4, 16)
        cp = pltpu.make_async_copy(q_ref.at[pl.ds(first, 16)], qs.at[e], sem.at[e])
        cp.start()
        copies.append(cp)
    gy = meta_ref[0] & (NY - 1)
    row = lax.broadcasted_iota(jnp.int32, (16, 2 * TILE * HD), 0)
    for e in range(3):
        copies[e].wait()
        block = qs[e].astype(jnp.float32)
        one = jnp.sum(jnp.where(row == (xrow[e] & 15), block, 0.0), axis=0, keepdims=True)
        for t in range(2):
            parts = [one[:, (t * TILE + c) * HD:(t * TILE + c + 1) * HD] for c in range(TILE)]
            out_ref[gy, NZ * PER + e * 3 + 1 + t] = jnp.concatenate(parts, axis=0).astype(BF)


def pack_kv(me, rg, kv, q):
    return pl.pallas_call(
        pack_kv_kernel,
        out_shape=(
            jax.ShapeDtypeStruct((NY, NZ * PER + EXT, TILE, HD), BF),
            jax.ShapeDtypeStruct((ROWS,), jnp.int32),
            jax.ShapeDtypeStruct((8,), jnp.int32),
        ),
        in_specs=[SM, SM, VM, ANY],
        out_specs=(VM, SM, SM),
        scratch_shapes=[
            pltpu.SMEM((NZ * NY,), jnp.int32),
            pltpu.SMEM((4,), jnp.int32),
            pltpu.VMEM((3, 16, 2 * TILE * HD), BF),
            pltpu.SemaphoreType.DMA((3,)),
        ],
        compiler_params=params(),
        name="pack_kv",
    )(me, rg, kv, q)


def assemble_kv_kernel(sc_ref, yr_ref, out_ref):
    ysrc = sc_ref[0]
    for z in range(NZ):
        for y in range(NY):
            out_ref[z, y * PER:(y + 1) * PER] = yr_ref[y, z * PER:(z + 1) * PER]
        if z < EXT:
            out_ref[z, NY * PER] = yr_ref[ysrc, NZ * PER + z]
        else:
            out_ref[z, NY * PER] = jnp.zeros((TILE, HD), BF)


def assemble_kv(sc, yr):
    return pl.pallas_call(
        assemble_kv_kernel,
        out_shape=jax.ShapeDtypeStruct((NZ, NY * PER + 1, TILE, HD), BF),
        in_specs=[SM, VM],
        out_specs=VM,
        compiler_params=params(),
        name="assemble_kv",
    )(sc, yr)


def pack_q_kernel(slot_ref, q_ref, a_ref, b_ref):
    a_ref[...] = jnp.zeros_like(a_ref)
    b_ref[...] = jnp.zeros_like(b_ref)

    def step(i, carry):
        s = slot_ref[i]

        @pl.when(s < ROWS)
        def _():
            a_ref[s] = q_ref[i, 0:TILE]
            b_ref[s] = q_ref[i, TILE:2 * TILE]

        return carry

    lax.fori_loop(0, ROWS, step, 0, unroll=8)


def pack_q(slot, q3):
    shape = jax.ShapeDtypeStruct((ROWS, TILE, HD), BF)
    return pl.pallas_call(
        pack_q_kernel,
        out_shape=(shape, shape),
        in_specs=[SM, VM],
        out_specs=(VM, VM),
        compiler_params=params(),
        name="pack_q",
    )(slot, q3)


def assemble_q_hop_kernel(sc_ref, b0, b1, b2, b3, hop_ref, out_ref):
    dz = sc_ref[1]
    for z in range(NZ):
        for k, b in enumerate((b0, b1, b2, b3)):
            out_ref[z, k * PER:(k + 1) * PER] = b[z * PER:(z + 1) * PER]
        out_ref[z, NY * PER] = hop_ref[(z - dz) & (NZ - 1), 0]


def assemble_q_hop(sc, blocks, zr1):
    whole = lambda n: pl.BlockSpec((n, TILE, HD), lambda i: (0, 0, 0))
    return pl.pallas_call(
        assemble_q_hop_kernel,
        grid=(1,),
        out_shape=jax.ShapeDtypeStruct((NZ, NY * PER + 1, TILE, HD), BF),
        in_specs=[SM] + [whole(NZ * PER)] * NY
        + [pl.BlockSpec((NZ, 1, TILE, HD), lambda i: (0, NY * PER, 0, 0))],
        out_specs=pl.BlockSpec((NZ, NY * PER + 1, TILE, HD), lambda i: (0, 0, 0, 0)),
        compiler_params=params(),
        name="assemble_q_hop",
    )(sc, *blocks, zr1)


def unpack_kernel(part, limit, idx_ref, src_ref, hop_ref, out_ref):
    def step(p, carry):
        i = idx_ref[p]
        over = i >= limit
        base = src_ref[jnp.where(over, 0, i)]
        ext = hop_ref[jnp.where(over, (i - limit) * 3 + part, 0), 0]
        out_ref[p] = jnp.where(over, ext, base)
        return carry

    lax.fori_loop(0, ROWS, step, 0, unroll=8)


def unpack(part, idx, zr, zr2):
    limit = zr.shape[0] * zr.shape[1]
    return pl.pallas_call(
        functools.partial(unpack_kernel, part, limit),
        grid=(1,),
        out_shape=jax.ShapeDtypeStruct((ROWS, TILE, HD), BF),
        in_specs=[
            SM,
            pl.BlockSpec((limit, TILE, HD), lambda i: (0, 0, 0)),
            pl.BlockSpec((NZ, 1, TILE, HD), lambda i: (0, NY * PER, 0, 0)),
        ],
        out_specs=pl.BlockSpec((ROWS, TILE, HD), lambda i: (0, 0, 0)),
        compiler_params=params(),
        name="unpack",
    )(idx, zr.reshape(limit, TILE, HD), zr2)


def attend_kernel(scale, q_ref, kv_ref, segq_ref, segk_ref, *rest):
    out_ref = rest[-1]
    half = ROWS // 2
    for b in range(2):
        lo, width = b * half, ROWS * 2 + half
        segq = segq_ref[lo:lo + half, :]
        segk = segk_ref[:, lo:lo + width]
        i = lax.broadcasted_iota(jnp.int32, (half, width), 0)
        j = lax.broadcasted_iota(jnp.int32, (half, width), 1)
        seen = (segq == segk) & (j <= i + 2 * ROWS)
        keys = kv_ref[0, lo:lo + width, :]
        values = kv_ref[1, lo:lo + width, :]
        for g in range(4):
            q = q_ref[g, lo:lo + half, :]
            s = lax.dot_general(q, keys, (((1,), (1,)), ((), ())), preferred_element_type=jnp.float32)
            s = jnp.where(seen, s * scale, -jnp.inf)
            w = jnp.exp(s - jnp.max(s, axis=1, keepdims=True))
            total = jnp.sum(w, axis=1, keepdims=True)
            o = jnp.dot(w.astype(BF), values, preferred_element_type=jnp.float32)
            out_ref[lo:lo + half, g * HD:(g + 1) * HD] = (o / total).astype(BF)


def attend(part, qt, kvt, segq, segk, prior=None):
    heads = TILE // 4
    in_specs = [
        pl.BlockSpec((4, ROWS, HD), lambda h: (h, 0, 0)),
        pl.BlockSpec((2, 3 * ROWS, HD), lambda h: (h + part * heads, 0, 0)),
        pl.BlockSpec((ROWS, 1), lambda h: (0, 0)),
        pl.BlockSpec((1, 3 * ROWS), lambda h: (0, 0)),
    ]
    args = [qt, kvt, segq, segk]
    alias = {}
    if prior is not None:
        in_specs.append(ANY)
        args.append(prior)
        alias = {4: 0}
    return pl.pallas_call(
        functools.partial(attend_kernel, HD ** -0.5),
        grid=(heads,),
        out_shape=jax.ShapeDtypeStruct((ROWS, 2 * TILE * HD), BF),
        in_specs=in_specs,
        out_specs=pl.BlockSpec((ROWS, 4 * HD), lambda h: (0, h + part * heads)),
        input_output_aliases=alias,
        compiler_params=params(),
        cost_estimate=pl.CostEstimate(
            flops=4 * ROWS * 480 * TILE * HD, bytes_accessed=4 << 20, transcendentals=ROWS * 480 * TILE
        ),
        name="attend",
    )(*args)


def on_device(queries, key_value, route_group, arrive_slot, segment_ids):
    z, y, s = lax.axis_index("z"), lax.axis_index("y"), lax.axis_index("seq")
    kv = key_value.reshape(ROWS, TILE, HD)
    up = lambda a, n: lax.ppermute(a, "seq", [(i, i + n) for i in range(NS - n)])

    seg = segment_ids.reshape(ROWS)
    seg1 = jnp.where(s >= 1, up(seg, 1), -1)
    seg2 = jnp.where(s >= 2, up(seg, 2), -1)
    segk = jnp.concatenate([seg2, seg1, seg])[None]
    segq = seg[:, None]

    src, rank = arrive_slot // 6, arrive_slot % 6
    sy, sz = src & (NY - 1), src >> 2
    over = rank >= PER
    dy = (y - sy) & (NY - 1)
    idx1 = jnp.where(over, NZ * 13 + rank - PER, sz * 13 + sy * PER + rank)
    idx2 = jnp.where(over, NZ * 13 + rank - PER, sz * 13 + dy * PER + rank)
    idx3 = jnp.where(over, NZ * 12 + rank - PER, sz * 12 + dy * PER + rank)

    yb, slot, meta = pack_kv(y.reshape(1), route_group, kv, queries)
    k6 = (meta[0] - (z * NY + y)) & (NZ * NY - 1)
    ysrc = (y - k6) & (NY - 1)
    dz = ((ysrc + k6) >> 2) & (NZ - 1)
    sc = jnp.stack([ysrc, dz]).astype(jnp.int32)

    yr = lax.all_to_all(yb, "y", 0, 0, tiled=True)
    zs1 = assemble_kv(sc, yr)
    zr1 = lax.all_to_all(zs1, "z", 0, 0, tiled=True)

    qa, qb = pack_q(slot, queries.reshape(ROWS, 2 * TILE, HD))

    def along_y(a):
        a = a.reshape(NY, NZ * PER, TILE, HD)
        return [a[0]] + [
            lax.ppermute(a[k], "y", [(i, (i + k) % NY) for i in range(NY)]) for k in range(1, NY)
        ]

    za, zb = along_y(qa), along_y(qb)
    zs3 = jnp.stack([b.reshape(NZ, PER, TILE, HD) for b in zb], axis=1).reshape(NZ, NY * PER, TILE, HD)

    zs2 = assemble_q_hop(sc, za, zr1)
    zr2 = lax.all_to_all(zs2, "z", 0, 0, tiled=True)
    zr3 = lax.all_to_all(zs3, "z", 0, 0, tiled=True)

    own = unpack(0, idx1, zr1, zr2)
    window = jnp.concatenate([up(own, 2), up(own, 1), own], axis=0)
    kvt = window.transpose(1, 0, 2)
    out = attend(0, unpack(1, idx2, zr2, zr2).transpose(1, 0, 2), kvt, segq, segk)
    return attend(1, unpack(2, idx3, zr3, zr2).transpose(1, 0, 2), kvt, segq, segk, out)


def solution(mesh):
    fine = Mesh(mesh.devices.reshape(NZ, NY, NS), ("z", "y", "seq"))
    rows = ("z", "y", "seq")
    return jax.shard_map(
        on_device,
        mesh=fine,
        in_specs=(
            P(rows, None),
            P(rows, None, None, None),
            P(rows),
            P(rows),
            P(("z", "y"), "seq"),
        ),
        out_specs=P(rows, None),
        check_vma=False,
    )
```

```python
import functools
import math

import jax
import jax.numpy as jnp
from jax import lax
from jax.experimental import pallas as pl
from jax.experimental.pallas import tpu as pltpu
from jax.sharding import Mesh, PartitionSpec as P

ROWS = 192
NZ, NY, NS = 16, 4, 8
PER = 3
TILE = 16
HD = 128
SLOT = NY * PER + 1
EXT = 9
BF = jnp.bfloat16
VMEM_LIMIT = 48 * 1024 * 1024

VM = pl.BlockSpec(memory_space=pltpu.VMEM)
SM = pl.BlockSpec(memory_space=pltpu.SMEM)
ANY = pl.BlockSpec(memory_space=pl.ANY)


def params(**kw):
    return pltpu.CompilerParams(vmem_limit_bytes=VMEM_LIMIT, **kw)


def pack_kv_kernel(me_ref, rg_ref, kv_ref, q_ref, out_ref, slot_ref, meta_ref, cnt, tile, xrow, kvs, qs, sem):
    load = pltpu.make_async_copy(kv_ref, kvs, sem.at[3])
    load.start()
    y = me_ref[0]
    for i in range(NZ * NY):
        cnt[i] = 0
    for e in range(4):
        xrow[e] = 0
    for e in range(8):
        meta_ref[e] = 0
    out_ref[...] = jnp.zeros_like(out_ref)

    def step(i, carry):
        d = rg_ref[i]
        r = cnt[d]
        cnt[d] = r + 1
        over = r >= PER
        dy, gz = ((d & (NY - 1)) - y) & (NY - 1), d >> 2
        tile[i] = jnp.where(over, (r - PER) * 3 * SLOT + SLOT - 1, gz * SLOT + dy * PER + r)
        slot_ref[i] = jnp.where(over, ROWS + r - PER, (dy * NZ + gz) * PER + r)

        @pl.when(over)
        def _():
            xrow[r - PER] = i
            meta_ref[0] = d

        return carry

    lax.fori_loop(0, ROWS, step, 0, unroll=8)
    copies = []
    for e in range(3):
        first = pl.multiple_of((xrow[e] >> 4) << 4, 16)
        cp = pltpu.make_async_copy(q_ref.at[pl.ds(first, 16)], qs.at[e], sem.at[e])
        cp.start()
        copies.append(cp)
    load.wait()

    def move(i, carry):
        out_ref[tile[i]] = kvs[i]
        return carry

    lax.fori_loop(0, ROWS, move, 0, unroll=8)
    row = lax.broadcasted_iota(jnp.int32, (16, 2 * TILE * HD), 0)
    for e in range(3):
        copies[e].wait()
        block = qs[e].astype(jnp.float32)
        one = jnp.sum(jnp.where(row == (xrow[e] & 15), block, 0.0), axis=0, keepdims=True)
        for t in range(2):
            parts = [one[:, (t * TILE + c) * HD:(t * TILE + c + 1) * HD] for c in range(TILE)]
            out_ref[(e * 3 + 1 + t) * SLOT + SLOT - 1] = jnp.concatenate(parts, axis=0).astype(BF)


def pack_kv(me, rg, kv, q):
    return pl.pallas_call(
        pack_kv_kernel,
        out_shape=(
            jax.ShapeDtypeStruct((NZ * SLOT, TILE, HD), BF),
            jax.ShapeDtypeStruct((ROWS,), jnp.int32),
            jax.ShapeDtypeStruct((8,), jnp.int32),
        ),
        in_specs=[SM, SM, ANY, ANY],
        out_specs=(VM, SM, SM),
        scratch_shapes=[
            pltpu.SMEM((NZ * NY,), jnp.int32),
            pltpu.SMEM((ROWS,), jnp.int32),
            pltpu.SMEM((4,), jnp.int32),
            pltpu.VMEM((ROWS, TILE, HD), BF),
            pltpu.VMEM((3, 16, 2 * TILE * HD), BF),
            pltpu.SemaphoreType.DMA((4,)),
        ],
        compiler_params=params(),
        name="pack_kv",
    )(me, rg, kv, q)


def pack_q_kernel(slot_ref, q_ref, a_ref, b_ref):
    a_ref[...] = jnp.zeros_like(a_ref)
    b_ref[...] = jnp.zeros_like(b_ref)

    def step(i, carry):
        s = slot_ref[i]

        @pl.when(s < ROWS)
        def _():
            a_ref[s] = q_ref[i, 0:TILE]
            b_ref[s] = q_ref[i, TILE:2 * TILE]

        return carry

    lax.fori_loop(0, ROWS, step, 0, unroll=8)


def pack_q(slot, q3):
    shape = jax.ShapeDtypeStruct((ROWS, TILE, HD), BF)
    return pl.pallas_call(
        pack_q_kernel,
        out_shape=(shape, shape),
        in_specs=[SM, VM],
        out_specs=(VM, VM),
        compiler_params=params(),
        name="pack_q",
    )(slot, q3)


def assemble_q_hop_kernel(sc_ref, b0, b1, b2, b3, hop_ref, out_ref):
    dz = sc_ref[0]
    for z in range(NZ):
        for k, b in enumerate((b0, b1, b2, b3)):
            out_ref[z, k * PER:(k + 1) * PER] = b[z * PER:(z + 1) * PER]
        out_ref[z, NY * PER] = hop_ref[(z - dz) & (NZ - 1), 0]


def assemble_q_hop(sc, blocks, zr1):
    whole = lambda n: pl.BlockSpec((n, TILE, HD), lambda i: (0, 0, 0))
    return pl.pallas_call(
        assemble_q_hop_kernel,
        grid=(1,),
        out_shape=jax.ShapeDtypeStruct((NZ, NY * PER + 1, TILE, HD), BF),
        in_specs=[SM] + [whole(NZ * PER)] * NY
        + [pl.BlockSpec((NZ, 1, TILE, HD), lambda i: (0, NY * PER, 0, 0))],
        out_specs=pl.BlockSpec((NZ, NY * PER + 1, TILE, HD), lambda i: (0, 0, 0, 0)),
        compiler_params=params(),
        name="assemble_q_hop",
    )(sc, *blocks, zr1)


def unpack_kv_kernel(idx_ref, b0, b1, b2, b3, out_ref, held):
    for k, b in enumerate((b0, b1, b2, b3)):
        held[k * NZ * PER:(k + 1) * NZ * PER] = b[...]

    def step(p, carry):
        out_ref[p] = held[idx_ref[p]]
        return carry

    lax.fori_loop(0, ROWS, step, 0, unroll=8)


def unpack_kv(idx, blocks):
    return pl.pallas_call(
        unpack_kv_kernel,
        out_shape=jax.ShapeDtypeStruct((ROWS, TILE, HD), BF),
        in_specs=[SM] + [VM] * NY,
        out_specs=VM,
        scratch_shapes=[pltpu.VMEM((ROWS, TILE, HD), BF)],
        compiler_params=params(),
        name="unpack_kv",
    )(idx, *blocks)


def window_kernel(pos_ref, h2, h1, h0, e2, e1, e0, out_ref):
    for k, (h, e) in enumerate(((h2, e2), (h1, e1), (h0, e0))):
        out_ref[k * ROWS:(k + 1) * ROWS] = h[...]
        for i in range(3):
            out_ref[k * ROWS + pos_ref[k * 3 + i]] = e[i]


def window(pos, rows, extra):
    return pl.pallas_call(
        window_kernel,
        out_shape=jax.ShapeDtypeStruct((3 * ROWS, TILE, HD), BF),
        in_specs=[SM] + [VM] * 6,
        out_specs=VM,
        compiler_params=params(),
        name="window",
    )(pos, *rows, *extra)


def unpack_q_kernel(part, limit, idx_ref, src_ref, ext_ref, *rest):
    out_ref = rest[-1]

    def step(p, carry):
        i = idx_ref[p]
        over = i >= limit
        base = src_ref[jnp.where(over, 0, i)]
        ext = ext_ref[jnp.where(over, (i - limit) * 3 + part, 0)]
        out_ref[p] = jnp.where(over, ext, base)
        return carry

    lax.fori_loop(0, ROWS, step, 0, unroll=8)


def unpack_q(part, idx, zr, ext, *after):
    limit = zr.shape[0] * zr.shape[1]
    return pl.pallas_call(
        functools.partial(unpack_q_kernel, part, limit),
        out_shape=jax.ShapeDtypeStruct((ROWS, TILE, HD), BF),
        in_specs=[SM, VM, VM] + [ANY] * len(after),
        out_specs=VM,
        compiler_params=params(),
        name="unpack_q",
    )(idx, zr.reshape(limit, TILE, HD), ext, *after)


def attend_kernel(scale, q_ref, kv_ref, segq_ref, segk_ref, *rest):
    out_ref = rest[-1]
    span = 3 * ROWS
    i = lax.broadcasted_iota(jnp.int32, (ROWS, span), 0)
    j = lax.broadcasted_iota(jnp.int32, (ROWS, span), 1)
    seen = (segq_ref[...] == segk_ref[...]) & (j <= i + 2 * ROWS)
    q = q_ref[...].reshape(4 * ROWS, HD)
    s = lax.dot_general(q, kv_ref[0], (((1,), (1,)), ((), ())), preferred_element_type=jnp.float32)
    s = jnp.where(seen[None], s.reshape(4, ROWS, span), -jnp.inf).reshape(4 * ROWS, span)
    w = jnp.exp2((s - jnp.max(s, axis=1, keepdims=True)) * (scale * math.log2(math.e)))
    total = jnp.sum(w, axis=1, keepdims=True)
    o = jnp.dot(w.astype(BF), kv_ref[1], preferred_element_type=jnp.float32)
    o = (o / total).astype(BF)
    for g in range(4):
        out_ref[:, g * HD:(g + 1) * HD] = o[g * ROWS:(g + 1) * ROWS]


def attend(part, qt, kvt, segq, segk, prior=None):
    heads = TILE // 4
    in_specs = [
        pl.BlockSpec((4, ROWS, HD), lambda h: (h, 0, 0)),
        pl.BlockSpec((2, 3 * ROWS, HD), lambda h: (h + part * heads, 0, 0)),
        pl.BlockSpec((ROWS, 1), lambda h: (0, 0)),
        pl.BlockSpec((1, 3 * ROWS), lambda h: (0, 0)),
    ]
    args = [qt, kvt, segq, segk]
    alias = {}
    if prior is not None:
        in_specs.append(ANY)
        args.append(prior)
        alias = {4: 0}
    return pl.pallas_call(
        functools.partial(attend_kernel, HD ** -0.5),
        grid=(heads,),
        out_shape=jax.ShapeDtypeStruct((ROWS, 2 * TILE * HD), BF),
        in_specs=in_specs,
        out_specs=pl.BlockSpec((ROWS, 4 * HD), lambda h: (0, h + part * heads)),
        input_output_aliases=alias,
        compiler_params=params(),
        cost_estimate=pl.CostEstimate(
            flops=4 * ROWS * 576 * TILE * HD, bytes_accessed=4 << 20, transcendentals=ROWS * 576 * TILE
        ),
        name="attend",
    )(*args)


def on_device(queries, key_value, route_group, arrive_slot, segment_ids):
    z, y, s = lax.axis_index("z"), lax.axis_index("y"), lax.axis_index("seq")
    kv = key_value.reshape(ROWS, TILE, HD)
    up = lambda a, n: lax.ppermute(a, "seq", [(i, i + n) for i in range(NS - n)])
    side = lambda a, n: lax.ppermute(a, "y", [(i, (i + n) % NY) for i in range(NY)])

    src, rank = arrive_slot // 6, arrive_slot % 6
    sy, sz = src & (NY - 1), src >> 2
    over = rank >= PER
    dy = (y - sy) & (NY - 1)
    idx1 = jnp.where(over, 0, (dy * NZ + sz) * PER + rank)
    idx2 = jnp.where(over, NZ * SLOT + rank - PER, sz * SLOT + dy * PER + rank)
    idx3 = jnp.where(over, NZ * NY * PER + rank - PER, (sz * NY + dy) * PER + rank)

    place = jnp.arange(ROWS, dtype=jnp.int32)
    pos = jnp.stack([jnp.sum(jnp.where(rank == PER + e, place, 0)) for e in range(3)])
    note = jnp.concatenate([segment_ids.reshape(ROWS), pos])
    note1, note2 = up(note, 1), up(note, 2)
    seg = note[:ROWS]
    segk = jnp.concatenate(
        [jnp.where(s >= 2, note2[:ROWS], -1), jnp.where(s >= 1, note1[:ROWS], -1), seg]
    )[None]
    segq = seg[:, None]
    poses = jnp.concatenate([note2[ROWS:], note1[ROWS:], pos])

    zs1, slot, meta = pack_kv(y.reshape(1), route_group, kv, queries)
    k6 = (meta[0] - (z * NY + y)) & (NZ * NY - 1)
    dz = (((y + k6) >> 2) & (NZ - 1)).reshape(1)
    zr1 = lax.all_to_all(zs1.reshape(NZ, SLOT, TILE, HD), "z", 0, 0, tiled=True)

    qa, qb = pack_q(slot, queries.reshape(ROWS, 2 * TILE, HD))

    def along_y(a):
        a = a.reshape(NY, NZ * PER, TILE, HD)
        return [a[0]] + [side(a[k], k) for k in range(1, NY)]

    za, zb = along_y(qa), along_y(qb)
    za, zb = lax.optimization_barrier((za, zb))
    zs2 = assemble_q_hop(dz, za, zr1)
    zs3 = jnp.stack([b.reshape(NZ, PER, TILE, HD) for b in zb], axis=1).reshape(NZ, NY * PER, TILE, HD)
    zr2 = lax.all_to_all(zs2, "z", 0, 0, tiled=True)

    part = [zr1[:, k * PER:(k + 1) * PER].reshape(NZ * PER, TILE, HD) for k in range(NY)]
    own = unpack_kv(idx1, [part[0]] + [side(part[k], k) for k in range(1, NY)])
    own1, own2 = up(own, 1), up(own, 2)
    zs3, own1, own2 = lax.optimization_barrier((zs3, own1, own2))
    zr3 = lax.all_to_all(zs3, "z", 0, 0, tiled=True)

    came = zr2[:EXT, SLOT - 1]
    ext = jnp.stack([came] + [side(came, k) for k in range(1, NY)])
    ext = lax.dynamic_index_in_dim(ext, k6 & (NY - 1), 0, False)
    ext0 = ext.reshape(3, 3, TILE, HD)[:, 0]
    kvt = window(poses, (own2, own1, own), (up(ext0, 2), up(ext0, 1), ext0)).transpose(1, 0, 2)
    out = attend(0, unpack_q(1, idx2, zr2, ext).transpose(1, 0, 2), kvt, segq, segk)
    return attend(1, unpack_q(2, idx3, zr3, ext, out[:8, :HD]).transpose(1, 0, 2), kvt, segq, segk, out)


def solution(mesh):
    fine = Mesh(mesh.devices.reshape(NZ, NY, NS), ("z", "y", "seq"))
    rows = ("z", "y", "seq")
    return jax.shard_map(
        on_device,
        mesh=fine,
        in_specs=(
            P(rows, None),
            P(rows, None, None, None),
            P(rows),
            P(rows),
            P(("z", "y"), "seq"),
        ),
        out_specs=P(rows, None),
        check_vma=False,
    )
```

```python
import functools
import math

import jax
import jax.numpy as jnp
from jax import lax
from jax.experimental import pallas as pl
from jax.experimental.pallas import tpu as pltpu
from jax.sharding import Mesh, PartitionSpec as P

ROWS = 192
NZ, NY, NS = 16, 4, 8
PER = 3
TILE = 16
HD = 128
SLOT = NY * PER + 1
EXT = 9
BF = jnp.bfloat16
MIB = 1024 * 1024

VM = pl.BlockSpec(memory_space=pltpu.VMEM)
SM = pl.BlockSpec(memory_space=pltpu.SMEM)
HB = pl.BlockSpec(memory_space=pltpu.HBM)


def params(mib=16):
    return pltpu.CompilerParams(vmem_limit_bytes=mib * MIB)


def pack_kv_kernel(me_ref, rg_hbm, kv_hbm, q_hbm, out_ref, slot_ref, meta_ref, rg, cnt, tile, xrow, kvs, qs, sem, rsem):
    plan = pltpu.make_async_copy(rg_hbm, rg, rsem)
    plan.start()
    load = pltpu.make_async_copy(kv_hbm, kvs, sem.at[3])
    load.start()
    y = me_ref[0]
    for i in range(NZ * NY):
        cnt[i] = 0
    for e in range(4):
        xrow[e] = 0
    out_ref[...] = jnp.zeros_like(out_ref)
    plan.wait()

    def step(i, far):
        d = rg[i]
        r = cnt[d]
        cnt[d] = r + 1
        over = r >= PER
        dy, gz = ((d & (NY - 1)) - y) & (NY - 1), d >> 2
        tile[i] = jnp.where(over, (r - PER) * 3 * SLOT + SLOT - 1, gz * SLOT + dy * PER + r)
        slot_ref[i] = jnp.where(over, ROWS, (dy * NZ + gz) * PER + r)
        xrow[jnp.where(over, r - PER, 3)] = i
        return jnp.where(over, d, far)

    meta_ref[0] = lax.fori_loop(0, ROWS, step, 0, unroll=16)
    copies = []
    for e in range(3):
        first = pl.multiple_of((xrow[e] >> 4) << 4, 16)
        cp = pltpu.make_async_copy(q_hbm.at[pl.ds(first, 16)], qs.at[e], sem.at[e])
        cp.start()
        copies.append(cp)
    load.wait()

    def move(i, carry):
        out_ref[tile[i]] = kvs[i]
        return carry

    lax.fori_loop(0, ROWS, move, 0, unroll=16)
    row = lax.broadcasted_iota(jnp.int32, (16, 2 * TILE * HD), 0)
    for e in range(3):
        copies[e].wait()
        block = qs[e].astype(jnp.float32)
        one = jnp.sum(jnp.where(row == (xrow[e] & 15), block, 0.0), axis=0, keepdims=True)
        for t in range(2):
            parts = [one[:, (t * TILE + c) * HD:(t * TILE + c + 1) * HD] for c in range(TILE)]
            out_ref[(e * 3 + 1 + t) * SLOT + SLOT - 1] = jnp.concatenate(parts, axis=0).astype(BF)


def pack_kv(me, rg, kv, q):
    return pl.pallas_call(
        pack_kv_kernel,
        out_shape=(
            jax.ShapeDtypeStruct((NZ * SLOT, TILE, HD), BF),
            jax.ShapeDtypeStruct((ROWS,), jnp.int32),
            jax.ShapeDtypeStruct((1,), jnp.int32),
        ),
        in_specs=[SM, HB, HB, HB],
        out_specs=(VM, SM, SM),
        scratch_shapes=[
            pltpu.SMEM((ROWS,), jnp.int32),
            pltpu.SMEM((NZ * NY,), jnp.int32),
            pltpu.SMEM((ROWS,), jnp.int32),
            pltpu.SMEM((4,), jnp.int32),
            pltpu.VMEM((ROWS, TILE, HD), BF),
            pltpu.VMEM((3, 16, 2 * TILE * HD), BF),
            pltpu.SemaphoreType.DMA((4,)),
            pltpu.SemaphoreType.DMA,
        ],
        compiler_params=params(),
        name="pack_kv",
    )(me, rg, kv, q)


def pack_q_kernel(slot_ref, q_ref, a_ref, b_ref):
    a_ref[...] = jnp.zeros_like(a_ref)
    b_ref[...] = jnp.zeros_like(b_ref)

    def step(i, carry):
        s = slot_ref[i]

        @pl.when(s < ROWS)
        def _():
            a_ref[s] = q_ref[i, 0:TILE]
            b_ref[s] = q_ref[i, TILE:2 * TILE]

        return carry

    lax.fori_loop(0, ROWS, step, 0, unroll=8)


def pack_q(slot, q3):
    shape = jax.ShapeDtypeStruct((ROWS, TILE, HD), BF)
    return pl.pallas_call(
        pack_q_kernel,
        out_shape=(shape, shape),
        in_specs=[SM, VM],
        out_specs=(VM, VM),
        compiler_params=params(),
        name="pack_q",
    )(slot, q3)


def assemble_q_hop_kernel(sc_ref, b0, b1, b2, b3, hop_ref, out_ref):
    dz = sc_ref[0]
    for z in range(NZ):
        for k, b in enumerate((b0, b1, b2, b3)):
            out_ref[z, k * PER:(k + 1) * PER] = b[z * PER:(z + 1) * PER]
        out_ref[z, NY * PER] = hop_ref[(z - dz) & (NZ - 1), 0]


def assemble_q_hop(sc, blocks, zr1):
    whole = lambda n: pl.BlockSpec((n, TILE, HD), lambda i: (0, 0, 0))
    return pl.pallas_call(
        assemble_q_hop_kernel,
        grid=(1,),
        out_shape=jax.ShapeDtypeStruct((NZ, NY * PER + 1, TILE, HD), BF),
        in_specs=[SM] + [whole(NZ * PER)] * NY
        + [pl.BlockSpec((NZ, 1, TILE, HD), lambda i: (0, NY * PER, 0, 0))],
        out_specs=pl.BlockSpec((NZ, NY * PER + 1, TILE, HD), lambda i: (0, 0, 0, 0)),
        compiler_params=params(),
        name="assemble_q_hop",
    )(sc, *blocks, zr1)


def unpack_kv_kernel(idx_ref, b0, b1, b2, b3, out_ref, held):
    for k, b in enumerate((b0, b1, b2, b3)):
        held[k * NZ * PER:(k + 1) * NZ * PER] = b[...]

    def step(p, carry):
        out_ref[p] = held[idx_ref[p]]
        return carry

    lax.fori_loop(0, ROWS, step, 0, unroll=8)


def unpack_kv(idx, blocks):
    return pl.pallas_call(
        unpack_kv_kernel,
        out_shape=jax.ShapeDtypeStruct((ROWS, TILE, HD), BF),
        in_specs=[SM] + [VM] * NY,
        out_specs=VM,
        scratch_shapes=[pltpu.VMEM((ROWS, TILE, HD), BF)],
        compiler_params=params(),
        name="unpack_kv",
    )(idx, *blocks)


def window_kernel(pos_ref, h2, h1, h0, e2, e1, e0, out_ref):
    for k, (h, e) in enumerate(((h2, e2), (h1, e1), (h0, e0))):
        out_ref[k * ROWS:(k + 1) * ROWS] = h[...]
        for i in range(3):
            out_ref[k * ROWS + pos_ref[k * 3 + i]] = e[i]


def window(pos, rows, extra):
    return pl.pallas_call(
        window_kernel,
        out_shape=jax.ShapeDtypeStruct((3 * ROWS, TILE, HD), BF),
        in_specs=[SM] + [VM] * 6,
        out_specs=VM,
        compiler_params=params(),
        name="window",
    )(pos, *rows, *extra)


def unpack_q_kernel(part, idx_ref, pos_ref, src_ref, ext_ref, *rest):
    out_ref = rest[-1]

    def step(p, carry):
        out_ref[p] = src_ref[idx_ref[p]]
        return carry

    lax.fori_loop(0, ROWS, step, 0, unroll=16)
    for e in range(3):
        out_ref[pos_ref[e]] = ext_ref[e * 3 + part]


def unpack_q(part, idx, pos, zr, ext, *after):
    return pl.pallas_call(
        functools.partial(unpack_q_kernel, part),
        out_shape=jax.ShapeDtypeStruct((ROWS, TILE, HD), BF),
        in_specs=[SM, SM, VM, VM] + [VM] * len(after),
        out_specs=VM,
        compiler_params=params(),
        name="unpack_q",
    )(idx, pos, zr.reshape(-1, TILE, HD), ext, *after)


def attend_kernel(part, scale, q_ref, kv_ref, segq_ref, segk_ref, *rest):
    out_hbm, held, sem = rest[-3:]
    heads = TILE // 4
    blocks = []
    for lo, rows in ((0, 128), (128, 64)):
        span = min(rows + 2 * ROWS, 3 * ROWS - lo)
        i = lax.broadcasted_iota(jnp.int32, (rows, span), 0)
        j = lax.broadcasted_iota(jnp.int32, (rows, span), 1)
        seen = (segq_ref[lo:lo + rows, :] == segk_ref[:, lo:lo + span]) & (j <= i + 2 * ROWS)
        blocks.append((lo, rows, span, seen))
    copies = []
    for h in range(heads):
        k = 2 * (part * heads + h)
        for lo, rows, span, seen in blocks:
            q = q_ref[4 * h:4 * h + 4, lo:lo + rows].reshape(4 * rows, HD)
            s = lax.dot_general(
                q, kv_ref[k, lo:lo + span], (((1,), (1,)), ((), ())), preferred_element_type=jnp.float32
            )
            s = jnp.where(seen[None], s.reshape(4, rows, span), -jnp.inf).reshape(4 * rows, span)
            w = jnp.exp2((s - jnp.max(s, axis=1, keepdims=True)) * (scale * math.log2(math.e)))
            total = jnp.sum(w, axis=1, keepdims=True)
            o = jnp.dot(w.astype(BF), kv_ref[k + 1, lo:lo + span], preferred_element_type=jnp.float32)
            o = (o / total).astype(BF)
            for g in range(4):
                held[h, lo:lo + rows, g * HD:(g + 1) * HD] = o[g * rows:(g + 1) * rows]
        first = (part * heads + h) * 4 * HD
        cp = pltpu.make_async_copy(held.at[h], out_hbm.at[:, first:first + 4 * HD], sem.at[h])
        cp.start()
        copies.append(cp)
    for cp in copies:
        cp.wait()


def attend(part, qt, kvt, segq, segk, *prior):
    heads = TILE // 4
    return pl.pallas_call(
        functools.partial(attend_kernel, part, HD ** -0.5),
        out_shape=jax.ShapeDtypeStruct((ROWS, 2 * TILE * HD), BF),
        in_specs=[VM] * 4 + [HB] * len(prior),
        out_specs=HB,
        scratch_shapes=[pltpu.VMEM((heads, ROWS, 4 * HD), BF), pltpu.SemaphoreType.DMA((heads,))],
        input_output_aliases={4: 0} if prior else {},
        compiler_params=params(32),
        cost_estimate=pl.CostEstimate(
            flops=4 * ROWS * 576 * TILE * HD, bytes_accessed=4 << 20, transcendentals=ROWS * 576 * TILE
        ),
        name="attend",
    )(qt, kvt, segq, segk, *prior)


def on_device(queries, key_value, route_group, arrive_slot, segment_ids):
    z, y, s = lax.axis_index("z"), lax.axis_index("y"), lax.axis_index("seq")
    kv = key_value.reshape(ROWS, TILE, HD)
    up = lambda a, n: lax.ppermute(a, "seq", [(i, i + n) for i in range(NS - n)])
    side = lambda a, n: lax.ppermute(a, "y", [(i, (i + n) % NY) for i in range(NY)])

    src, rank = arrive_slot // 6, arrive_slot % 6
    sy, sz = src & (NY - 1), src >> 2
    over = rank >= PER
    dy = (y - sy) & (NY - 1)
    idx1 = jnp.where(over, 0, (dy * NZ + sz) * PER + rank)
    idx2 = jnp.where(over, 0, sz * SLOT + dy * PER + rank)
    idx3 = jnp.where(over, 0, (sz * NY + dy) * PER + rank)

    place = jnp.arange(ROWS, dtype=jnp.int32)
    pos = jnp.stack([jnp.sum(jnp.where(rank == PER + e, place, 0)) for e in range(3)])
    note = jnp.concatenate([segment_ids.reshape(ROWS), pos])
    note1, note2 = up(note, 1), up(note, 2)

    zs1, slot, meta = pack_kv(y.reshape(1), route_group, kv, queries)
    k6 = (meta[0] - (z * NY + y)) & (NZ * NY - 1)
    dz = (((y + k6) >> 2) & (NZ - 1)).reshape(1)
    zr1 = lax.all_to_all(zs1.reshape(NZ, SLOT, TILE, HD), "z", 0, 0, tiled=True)

    qa, qb = pack_q(slot, queries.reshape(ROWS, 2 * TILE, HD))

    def along_y(a):
        a = a.reshape(NY, NZ * PER, TILE, HD)
        return [a[0]] + [side(a[k], k) for k in range(1, NY)]

    za, zb = along_y(qa), along_y(qb)
    za, zb, note1, note2 = lax.optimization_barrier((za, zb, note1, note2))
    seg = note[:ROWS]
    segk = jnp.concatenate(
        [jnp.where(s >= 2, note2[:ROWS], -1), jnp.where(s >= 1, note1[:ROWS], -1), seg]
    )[None]
    segq = seg[:, None]
    poses = jnp.concatenate([note2[ROWS:], note1[ROWS:], pos])

    zs2 = assemble_q_hop(dz, za, zr1)
    zs3 = jnp.stack([b.reshape(NZ, PER, TILE, HD) for b in zb], axis=1).reshape(NZ, NY * PER, TILE, HD)
    zr2 = lax.all_to_all(zs2, "z", 0, 0, tiled=True)

    part = [zr1[:, k * PER:(k + 1) * PER].reshape(NZ * PER, TILE, HD) for k in range(NY)]
    own = unpack_kv(idx1, [part[0]] + [side(part[k], k) for k in range(1, NY)])
    own2 = up(own, 2)
    zs3, own2 = lax.optimization_barrier((zs3, own2))
    own1 = lax.ppermute(jnp.where(s % 2 == 0, own, own2), "seq", [(i, i ^ 1) for i in range(NS)])
    zr3 = lax.all_to_all(zs3, "z", 0, 0, tiled=True)

    came = zr2[:EXT, SLOT - 1]
    ext = jnp.stack([came] + [side(came, k) for k in range(1, NY)])
    ext = lax.dynamic_index_in_dim(ext, k6 & (NY - 1), 0, False)
    ext0 = ext.reshape(3, 3, TILE, HD)[:, 0]
    kvt = window(poses, (own2, own1, own), (up(ext0, 2), up(ext0, 1), ext0)).transpose(1, 0, 2)
    out = attend(0, unpack_q(1, idx2, pos, zr2, ext).transpose(1, 0, 2), kvt, segq, segk)
    return attend(1, unpack_q(2, idx3, pos, zr3, ext, out[:8, :HD]).transpose(1, 0, 2), kvt, segq, segk, out)


def solution(mesh):
    fine = Mesh(mesh.devices.reshape(NZ, NY, NS), ("z", "y", "seq"))
    rows = ("z", "y", "seq")
    return jax.shard_map(
        on_device,
        mesh=fine,
        in_specs=(
            P(rows, None),
            P(rows, None, None, None),
            P(rows),
            P(rows),
            P(("z", "y"), "seq"),
        ),
        out_specs=P(rows, None),
        check_vma=False,
    )
```

```python
import functools
import math

import jax
import jax.numpy as jnp
from jax import lax
from jax.experimental import pallas as pl
from jax.experimental.pallas import tpu as pltpu
from jax.sharding import Mesh, PartitionSpec as P

ROWS = 192
NZ, NY, NS = 16, 4, 8
PER = 3
TILE = 16
HD = 128
SLOT = NY * PER + 1
EXT = 9
BF = jnp.bfloat16
MIB = 1024 * 1024

VM = pl.BlockSpec(memory_space=pltpu.VMEM)
SM = pl.BlockSpec(memory_space=pltpu.SMEM)
HB = pl.BlockSpec(memory_space=pltpu.HBM)


def params(mib=16):
    return pltpu.CompilerParams(vmem_limit_bytes=mib * MIB)


def pack_kv_kernel(me_ref, rg_hbm, kv_hbm, q_hbm, out_ref, slot_ref, meta_ref, rg, cnt, tile, xrow, kvs, qs, sem, rsem):
    plan = pltpu.make_async_copy(rg_hbm, rg, rsem)
    plan.start()
    load = pltpu.make_async_copy(kv_hbm, kvs, sem.at[3])
    load.start()
    y = me_ref[0]
    for i in range(NZ * NY):
        cnt[i] = 0
    for e in range(4):
        xrow[e] = 0
    out_ref[...] = jnp.zeros_like(out_ref)
    plan.wait()

    def step(i, far):
        d = rg[i]
        r = cnt[d]
        cnt[d] = r + 1
        over = r >= PER
        dy, gz = ((d & (NY - 1)) - y) & (NY - 1), d >> 2
        tile[i] = jnp.where(over, (r - PER) * 3 * SLOT + SLOT - 1, gz * SLOT + dy * PER + r)
        slot_ref[i] = jnp.where(over, ROWS, (dy * NZ + gz) * PER + r)
        xrow[jnp.where(over, r - PER, 3)] = i
        return jnp.where(over, d, far)

    meta_ref[0] = lax.fori_loop(0, ROWS, step, 0, unroll=16)
    copies = []
    for e in range(3):
        first = pl.multiple_of((xrow[e] >> 4) << 4, 16)
        cp = pltpu.make_async_copy(q_hbm.at[pl.ds(first, 16)], qs.at[e], sem.at[e])
        cp.start()
        copies.append(cp)
    load.wait()

    def move(i, carry):
        out_ref[tile[i]] = kvs[i]
        return carry

    lax.fori_loop(0, ROWS, move, 0, unroll=16)
    row = lax.broadcasted_iota(jnp.int32, (16, 2 * TILE * HD), 0)
    for e in range(3):
        copies[e].wait()
        block = qs[e].astype(jnp.float32)
        one = jnp.sum(jnp.where(row == (xrow[e] & 15), block, 0.0), axis=0, keepdims=True)
        for t in range(2):
            parts = [one[:, (t * TILE + c) * HD:(t * TILE + c + 1) * HD] for c in range(TILE)]
            out_ref[(e * 3 + 1 + t) * SLOT + SLOT - 1] = jnp.concatenate(parts, axis=0).astype(BF)


def pack_kv(me, rg, kv, q):
    return pl.pallas_call(
        pack_kv_kernel,
        out_shape=(
            jax.ShapeDtypeStruct((NZ * SLOT, TILE, HD), BF),
            jax.ShapeDtypeStruct((ROWS,), jnp.int32),
            jax.ShapeDtypeStruct((1,), jnp.int32),
        ),
        in_specs=[SM, HB, HB, HB],
        out_specs=(VM, SM, SM),
        scratch_shapes=[
            pltpu.SMEM((ROWS,), jnp.int32),
            pltpu.SMEM((NZ * NY,), jnp.int32),
            pltpu.SMEM((ROWS,), jnp.int32),
            pltpu.SMEM((4,), jnp.int32),
            pltpu.VMEM((ROWS, TILE, HD), BF),
            pltpu.VMEM((3, 16, 2 * TILE * HD), BF),
            pltpu.SemaphoreType.DMA((4,)),
            pltpu.SemaphoreType.DMA,
        ],
        compiler_params=params(60),
        name="pack_kv",
    )(me, rg, kv, q)


def pack_q_kernel(slot_ref, q_ref, a_ref, b_ref):
    a_ref[...] = jnp.zeros_like(a_ref)
    b_ref[...] = jnp.zeros_like(b_ref)

    def step(i, carry):
        s = slot_ref[i]
        a_ref[s] = q_ref[i, 0:TILE]
        b_ref[s] = q_ref[i, TILE:2 * TILE]
        return carry

    lax.fori_loop(0, ROWS, step, 0, unroll=16)


def pack_q(slot, q3):
    shape = jax.ShapeDtypeStruct((ROWS + 1, TILE, HD), BF)
    return pl.pallas_call(
        pack_q_kernel,
        out_shape=(shape, shape),
        in_specs=[SM, VM],
        out_specs=(VM, VM),
        compiler_params=params(),
        name="pack_q",
    )(slot, q3)


def assemble_q_hop_kernel(sc_ref, b0, b1, b2, b3, hop_ref, out_ref):
    dz = sc_ref[0]
    for z in range(NZ):
        for k, b in enumerate((b0, b1, b2, b3)):
            out_ref[z, k * PER:(k + 1) * PER] = b[z * PER:(z + 1) * PER]
        out_ref[z, NY * PER] = hop_ref[(z - dz) & (NZ - 1), 0]


def assemble_q_hop(sc, blocks, zr1):
    whole = lambda n: pl.BlockSpec((n, TILE, HD), lambda i: (0, 0, 0))
    return pl.pallas_call(
        assemble_q_hop_kernel,
        grid=(1,),
        out_shape=jax.ShapeDtypeStruct((NZ, NY * PER + 1, TILE, HD), BF),
        in_specs=[SM] + [whole(NZ * PER)] * NY
        + [pl.BlockSpec((NZ, 1, TILE, HD), lambda i: (0, NY * PER, 0, 0))],
        out_specs=pl.BlockSpec((NZ, NY * PER + 1, TILE, HD), lambda i: (0, 0, 0, 0)),
        compiler_params=params(),
        name="assemble_q_hop",
    )(sc, *blocks, zr1)


def unpack_kv_kernel(idx_ref, b0, b1, b2, b3, out_ref, held):
    for k, b in enumerate((b0, b1, b2, b3)):
        held[k * NZ * PER:(k + 1) * NZ * PER] = b[...]

    def step(p, carry):
        out_ref[p] = held[idx_ref[p]]
        return carry

    lax.fori_loop(0, ROWS, step, 0, unroll=8)


def unpack_kv(idx, blocks):
    return pl.pallas_call(
        unpack_kv_kernel,
        out_shape=jax.ShapeDtypeStruct((ROWS, TILE, HD), BF),
        in_specs=[SM] + [VM] * NY,
        out_specs=VM,
        scratch_shapes=[pltpu.VMEM((ROWS, TILE, HD), BF)],
        compiler_params=params(),
        name="unpack_kv",
    )(idx, *blocks)


def window_kernel(pos_ref, h2, h1a, h1b, h0, e2, e1, e0, out_ref):
    out_ref[:ROWS] = h2[...]
    out_ref[ROWS:2 * ROWS] = h1a[...] + h1b[...]
    out_ref[2 * ROWS:] = h0[...]
    for k, e in enumerate((e2, e1, e0)):
        for i in range(3):
            out_ref[k * ROWS + pos_ref[k * 3 + i]] = e[i]


def window(pos, rows, extra):
    return pl.pallas_call(
        window_kernel,
        out_shape=jax.ShapeDtypeStruct((3 * ROWS, TILE, HD), BF),
        in_specs=[SM] + [VM] * 7,
        out_specs=VM,
        compiler_params=params(),
        name="window",
    )(pos, *rows, *extra)


def unpack_q_kernel(part, idx_ref, pos_ref, src_ref, ext_ref, *rest):
    out_ref = rest[-1]

    def step(p, carry):
        out_ref[p] = src_ref[idx_ref[p]]
        return carry

    lax.fori_loop(0, ROWS, step, 0, unroll=16)
    for e in range(3):
        out_ref[pos_ref[e]] = ext_ref[e * 3 + part]


def unpack_q(part, idx, pos, zr, ext, *after):
    return pl.pallas_call(
        functools.partial(unpack_q_kernel, part),
        out_shape=jax.ShapeDtypeStruct((ROWS, TILE, HD), BF),
        in_specs=[SM, SM, VM, VM] + [VM] * len(after),
        out_specs=VM,
        compiler_params=params(),
        name="unpack_q",
    )(idx, pos, zr.reshape(-1, TILE, HD), ext, *after)


def attend_kernel(part, scale, q_ref, kv_ref, segq_ref, segk_ref, *rest):
    out_hbm, done_ref, held, sem = rest[-4:]
    done_ref[...] = jnp.zeros_like(done_ref)
    heads = TILE // 4
    blocks = []
    for lo, rows in ((0, 128), (128, 64)):
        span = min(rows + 2 * ROWS, 3 * ROWS - lo)
        i = lax.broadcasted_iota(jnp.int32, (rows, span), 0)
        j = lax.broadcasted_iota(jnp.int32, (rows, span), 1)
        seen = (segq_ref[lo:lo + rows, :] == segk_ref[:, lo:lo + span]) & (j <= i + 2 * ROWS)
        blocks.append((lo, rows, span, seen))
    copies = []
    for h in range(heads):
        k = 2 * (part * heads + h)
        for lo, rows, span, seen in blocks:
            q = q_ref[4 * h:4 * h + 4, lo:lo + rows].reshape(4 * rows, HD)
            s = lax.dot_general(
                q, kv_ref[k, lo:lo + span], (((1,), (1,)), ((), ())), preferred_element_type=jnp.float32
            )
            s = jnp.where(seen[None], s.reshape(4, rows, span), -jnp.inf).reshape(4 * rows, span)
            w = jnp.exp2((s - jnp.max(s, axis=1, keepdims=True)) * (scale * math.log2(math.e)))
            total = jnp.sum(w, axis=1, keepdims=True)
            o = jnp.dot(w.astype(BF), kv_ref[k + 1, lo:lo + span], preferred_element_type=jnp.float32)
            o = (o / total).astype(BF)
            for g in range(4):
                held[h, lo:lo + rows, g * HD:(g + 1) * HD] = o[g * rows:(g + 1) * rows]
        first = (part * heads + h) * 4 * HD
        cp = pltpu.make_async_copy(held.at[h], out_hbm.at[:, first:first + 4 * HD], sem.at[h])
        cp.start()
        copies.append(cp)
    for cp in copies:
        cp.wait()


def attend(part, qt, kvt, segq, segk, *prior):
    heads = TILE // 4
    return pl.pallas_call(
        functools.partial(attend_kernel, part, HD ** -0.5),
        out_shape=(
            jax.ShapeDtypeStruct((ROWS, 2 * TILE * HD), BF),
            jax.ShapeDtypeStruct((8, HD), jnp.float32),
        ),
        in_specs=[VM] * 4 + [HB] * len(prior),
        out_specs=(HB, VM),
        scratch_shapes=[pltpu.VMEM((heads, ROWS, 4 * HD), BF), pltpu.SemaphoreType.DMA((heads,))],
        input_output_aliases={4: 0} if prior else {},
        compiler_params=params(32),
        cost_estimate=pl.CostEstimate(
            flops=4 * ROWS * 576 * TILE * HD, bytes_accessed=4 << 20, transcendentals=ROWS * 576 * TILE
        ),
        name="attend",
    )(qt, kvt, segq, segk, *prior)


def on_device(queries, key_value, route_group, arrive_slot, segment_ids):
    z, y, s = lax.axis_index("z"), lax.axis_index("y"), lax.axis_index("seq")
    kv = key_value.reshape(ROWS, TILE, HD)
    up = lambda a, n: lax.ppermute(a, "seq", [(i, i + n) for i in range(NS - n)])
    side = lambda a, n: lax.ppermute(a, "y", [(i, (i + n) % NY) for i in range(NY)])

    src, rank = arrive_slot // 6, arrive_slot % 6
    sy, sz = src & (NY - 1), src >> 2
    over = rank >= PER
    dy = (y - sy) & (NY - 1)
    idx1 = jnp.where(over, 0, (dy * NZ + sz) * PER + rank)
    idx2 = jnp.where(over, 0, sz * SLOT + dy * PER + rank)
    idx3 = jnp.where(over, 0, (sz * NY + dy) * PER + rank)

    place = jnp.arange(ROWS, dtype=jnp.int32)
    pos = jnp.stack([jnp.sum(jnp.where(rank == PER + e, place, 0)) for e in range(3)])
    note = jnp.concatenate([segment_ids.reshape(ROWS), pos])
    note1, note2 = up(note, 1), up(note, 2)

    zs1, slot, meta = pack_kv(y.reshape(1), route_group, kv, queries)
    k6 = (meta[0] - (z * NY + y)) & (NZ * NY - 1)
    dz = (((y + k6) >> 2) & (NZ - 1)).reshape(1)
    zr1 = lax.all_to_all(zs1.reshape(NZ, SLOT, TILE, HD), "z", 0, 0, tiled=True)

    slot, queries = lax.optimization_barrier((slot, queries))
    qa, qb = pack_q(slot, queries.reshape(ROWS, 2 * TILE, HD))

    def along_y(a):
        n = NZ * PER
        return [a[:n]] + [side(a[k * n:(k + 1) * n], k) for k in range(1, NY)]

    za, zb = along_y(qa), along_y(qb)
    seg = note[:ROWS]
    segk = jnp.concatenate(
        [jnp.where(s >= 2, note2[:ROWS], -1), jnp.where(s >= 1, note1[:ROWS], -1), seg]
    )[None]
    segq = seg[:, None]
    poses = jnp.concatenate([note2[ROWS:], note1[ROWS:], pos])
    small = (segk, segq, poses, pos, idx1, idx2, idx3, k6, dz)
    za, zb, small = lax.optimization_barrier((za, zb, small))
    segk, segq, poses, pos, idx1, idx2, idx3, k6, dz = small

    zs2 = assemble_q_hop(dz, za, zr1)
    zs3 = jnp.stack([b.reshape(NZ, PER, TILE, HD) for b in zb], axis=1).reshape(NZ, NY * PER, TILE, HD)
    zr2 = lax.all_to_all(zs2, "z", 0, 0, tiled=True)

    part = [zr1[:, k * PER:(k + 1) * PER].reshape(NZ * PER, TILE, HD) for k in range(NY)]
    own = unpack_kv(idx1, [part[0]] + [side(part[k], k) for k in range(1, NY)])
    own2 = up(own, 2)
    own1a = lax.ppermute(own, "seq", [(i, i + 1) for i in range(0, NS, 2)])
    zs3, own2, own1a = lax.optimization_barrier((zs3, own2, own1a))
    own1b = lax.ppermute(own2, "seq", [(i + 1, i) for i in range(0, NS, 2)])
    zr3 = lax.all_to_all(zs3, "z", 0, 0, tiled=True)

    came = zr2[:EXT, SLOT - 1]
    ext = jnp.stack([came] + [side(came, k) for k in range(1, NY)])
    ext = lax.dynamic_index_in_dim(ext, k6 & (NY - 1), 0, False)
    ext0 = ext.reshape(3, 3, TILE, HD)[:, 0]
    kvt = window(poses, (own2, own1a, own1b, own), (up(ext0, 2), up(ext0, 1), ext0)).transpose(1, 0, 2)
    out, done = attend(0, unpack_q(1, idx2, pos, zr2, ext).transpose(1, 0, 2), kvt, segq, segk)
    return attend(1, unpack_q(2, idx3, pos, zr3, ext, done).transpose(1, 0, 2), kvt, segq, segk, out)[0]


def solution(mesh):
    fine = Mesh(mesh.devices.reshape(NZ, NY, NS), ("z", "y", "seq"))
    rows = ("z", "y", "seq")
    return jax.shard_map(
        on_device,
        mesh=fine,
        in_specs=(
            P(rows, None),
            P(rows, None, None, None),
            P(rows),
            P(rows),
            P(("z", "y"), "seq"),
        ),
        out_specs=P(rows, None),
        check_vma=False,
    )
```

```python
import functools
import math

import jax
import jax.numpy as jnp
from jax import lax
from jax.experimental import pallas as pl
from jax.experimental.pallas import tpu as pltpu
from jax.sharding import Mesh, PartitionSpec as P

ROWS = 192
NZ, NY, NS = 16, 4, 8
PER = 3
TILE = 16
HD = 128
SLOT = NY * PER + 1
EXT = 9
BF = jnp.bfloat16
MIB = 1024 * 1024

VM = pl.BlockSpec(memory_space=pltpu.VMEM)
SM = pl.BlockSpec(memory_space=pltpu.SMEM)
HB = pl.BlockSpec(memory_space=pltpu.HBM)


def params(mib=16):
    return pltpu.CompilerParams(vmem_limit_bytes=mib * MIB)


def pack_kv_kernel(me_ref, rg_hbm, kv_hbm, q_hbm, out_ref, tile_ref, meta_ref, rg, nxt, xrow, kvs, qs, sem):
    plan = pltpu.make_async_copy(rg_hbm, rg, sem.at[0])
    plan.start()
    load = pltpu.make_async_copy(kv_hbm, kvs, sem.at[1])
    load.start()
    load_q = pltpu.make_async_copy(q_hbm, qs, sem.at[2])
    load_q.start()
    y = me_ref[0]
    for d in range(NZ * NY):
        nxt[d] = (d // NY * SLOT + ((d % NY - y) & (NY - 1)) * PER) * 8
    for e in range(4):
        xrow[e] = 0
    out_ref[...] = jnp.zeros_like(out_ref)
    plan.wait()

    def step(i, far):
        d = rg[i]
        n = nxt[d]
        r = n & 7
        nxt[d] = n + 9
        over = r >= PER
        tile_ref[i] = jnp.where(over, (r - PER) * 3 * SLOT + SLOT - 1, n >> 3)
        xrow[jnp.where(over, r - PER, 3)] = i
        return jnp.where(over, d, far)

    meta_ref[0] = lax.fori_loop(0, ROWS, step, 0, unroll=16)
    load.wait()

    def move(i, carry):
        out_ref[tile_ref[i]] = kvs[i]
        return carry

    lax.fori_loop(0, ROWS, move, 0, unroll=16)
    load_q.wait()
    row = lax.broadcasted_iota(jnp.int32, (16, 2 * TILE * HD), 0)
    for e in range(3):
        first = pl.multiple_of((xrow[e] >> 4) << 4, 16)
        block = qs[pl.ds(first, 16), :].astype(jnp.float32)
        one = jnp.sum(jnp.where(row == (xrow[e] & 15), block, 0.0), axis=0, keepdims=True)
        for t in range(2):
            parts = [one[:, (t * TILE + c) * HD:(t * TILE + c + 1) * HD] for c in range(TILE)]
            out_ref[(e * 3 + 1 + t) * SLOT + SLOT - 1] = jnp.concatenate(parts, axis=0).astype(BF)


def pack_kv(me, rg, kv, q):
    return pl.pallas_call(
        pack_kv_kernel,
        out_shape=(
            jax.ShapeDtypeStruct((NZ * SLOT, TILE, HD), BF),
            jax.ShapeDtypeStruct((ROWS,), jnp.int32),
            jax.ShapeDtypeStruct((1,), jnp.int32),
        ),
        in_specs=[SM, HB, HB, HB],
        out_specs=(VM, SM, SM),
        scratch_shapes=[
            pltpu.SMEM((ROWS,), jnp.int32),
            pltpu.SMEM((NZ * NY,), jnp.int32),
            pltpu.SMEM((4,), jnp.int32),
            pltpu.VMEM((ROWS, TILE, HD), BF),
            pltpu.VMEM((ROWS, 2 * TILE * HD), BF),
            pltpu.SemaphoreType.DMA((3,)),
        ],
        compiler_params=params(60),
        name="pack_kv",
    )(me, rg, kv, q)


def pack_q_kernel(tile_ref, q_ref, out_ref):
    out_ref[...] = jnp.zeros_like(out_ref)

    def step(i, carry):
        t = tile_ref[i]
        gz = (t * 79) >> 10
        k = t - gz * SLOT
        dy = (k * 11) >> 5
        out_ref[jnp.where(k == SLOT - 1, ROWS, (dy * NZ + gz) * PER + k - dy * PER)] = q_ref[i]
        return carry

    lax.fori_loop(0, ROWS, step, 0, unroll=16)


def pack_q(tile, q3):
    return pl.pallas_call(
        pack_q_kernel,
        out_shape=jax.ShapeDtypeStruct((ROWS + 1, 2 * TILE, HD), BF),
        in_specs=[SM, VM],
        out_specs=VM,
        compiler_params=params(),
        name="pack_q",
    )(tile, q3)


def assemble_a_kernel(dz_ref, b0, b1, b2, b3, hop_ref, out_ref):
    dz = dz_ref[0]
    for z in range(NZ):
        for k, b in enumerate((b0, b1, b2, b3)):
            out_ref[z, k * PER:(k + 1) * PER] = b[z * PER:(z + 1) * PER, :TILE]
        out_ref[z, NY * PER] = hop_ref[(z - dz) & (NZ - 1), 0]


def assemble_a(dz, blocks, zr1):
    whole = pl.BlockSpec((NZ * PER, 2 * TILE, HD), lambda i: (0, 0, 0))
    return pl.pallas_call(
        assemble_a_kernel,
        grid=(1,),
        out_shape=jax.ShapeDtypeStruct((NZ, SLOT, TILE, HD), BF),
        in_specs=[SM] + [whole] * NY + [pl.BlockSpec((NZ, 1, TILE, HD), lambda i: (0, SLOT - 1, 0, 0))],
        out_specs=pl.BlockSpec((NZ, SLOT, TILE, HD), lambda i: (0, 0, 0, 0)),
        compiler_params=params(),
        name="assemble_a",
    )(dz, *blocks, zr1)


def assemble_b_kernel(b0, b1, b2, b3, out_ref):
    for z in range(NZ):
        for k, b in enumerate((b0, b1, b2, b3)):
            out_ref[z, k * PER:(k + 1) * PER] = b[z * PER:(z + 1) * PER, TILE:]


def assemble_b(blocks):
    return pl.pallas_call(
        assemble_b_kernel,
        out_shape=jax.ShapeDtypeStruct((NZ, NY * PER, TILE, HD), BF),
        in_specs=[VM] * NY,
        out_specs=VM,
        compiler_params=params(),
        name="assemble_b",
    )(*blocks)


def unpack_kv_kernel(idx_ref, b0, b1, b2, b3, out_ref, held):
    for k, b in enumerate((b0, b1, b2, b3)):
        held[k * NZ * PER:(k + 1) * NZ * PER] = b[...]

    def step(p, carry):
        out_ref[p] = held[idx_ref[p]]
        return carry

    lax.fori_loop(0, ROWS, step, 0, unroll=8)


def unpack_kv(idx, blocks):
    return pl.pallas_call(
        unpack_kv_kernel,
        out_shape=jax.ShapeDtypeStruct((ROWS, TILE, HD), BF),
        in_specs=[SM] + [VM] * NY,
        out_specs=VM,
        scratch_shapes=[pltpu.VMEM((ROWS, TILE, HD), BF)],
        compiler_params=params(),
        name="unpack_kv",
    )(idx, *blocks)


def window_kernel(at_ref, n2, n1, n0, m2, m1, m0, h2, h1a, h1b, h0, e2, e1, e0, out_ref, seg_ref):
    out_ref[:ROWS] = h2[...]
    out_ref[ROWS:2 * ROWS] = h1a[...] + h1b[...]
    out_ref[2 * ROWS:] = h0[...]
    for k, (n, e) in enumerate(((n2, e2), (n1, e1), (n0, e0))):
        for i in range(3):
            out_ref[k * ROWS + n[ROWS + i]] = e[i]
    at = at_ref[0]
    seg_ref[:, :ROWS] = jnp.where(at >= 2, m2[:, :ROWS], -1)
    seg_ref[:, ROWS:2 * ROWS] = jnp.where(at >= 1, m1[:, :ROWS], -1)
    seg_ref[:, 2 * ROWS:] = m0[:, :ROWS]


def window(at, notes, rows, extra):
    return pl.pallas_call(
        window_kernel,
        out_shape=(
            jax.ShapeDtypeStruct((3 * ROWS, TILE, HD), BF),
            jax.ShapeDtypeStruct((1, 3 * ROWS), jnp.int32),
        ),
        in_specs=[SM] * 4 + [VM] * 10,
        out_specs=(VM, VM),
        compiler_params=params(),
        name="window",
    )(at, *notes, *[n[None] for n in notes], *rows, *extra)


def unpack_q_kernel(part, idx_ref, note_ref, src_ref, ext_ref, *rest):
    out_ref = rest[-1]

    def step(p, carry):
        out_ref[p] = src_ref[idx_ref[p]]
        return carry

    lax.fori_loop(0, ROWS, step, 0, unroll=16)
    for e in range(3):
        out_ref[note_ref[ROWS + e]] = ext_ref[e * 3 + part]


def unpack_q(part, idx, note, zr, ext, *after):
    return pl.pallas_call(
        functools.partial(unpack_q_kernel, part),
        out_shape=jax.ShapeDtypeStruct((ROWS, TILE, HD), BF),
        in_specs=[SM, SM, VM, VM] + [VM] * len(after),
        out_specs=VM,
        compiler_params=params(),
        name="unpack_q",
    )(idx, note, zr.reshape(-1, TILE, HD), ext, *after)


def attend_kernel(part, scale, q_ref, kv_ref, segq_ref, segk_ref, *rest):
    if part == 0:
        out_hbm, done_ref, held, sem = rest
        done_ref[...] = jnp.zeros_like(done_ref)
    else:
        _, out_hbm, held, sem = rest
    heads = TILE // 4
    blocks = []
    for lo, rows in ((0, 128), (128, 64)):
        span = min(rows + 2 * ROWS, 3 * ROWS - lo)
        i = lax.broadcasted_iota(jnp.int32, (rows, span), 0)
        j = lax.broadcasted_iota(jnp.int32, (rows, span), 1)
        seen = (segq_ref[lo:lo + rows, :] == segk_ref[:, lo:lo + span]) & (j <= i + 2 * ROWS)
        blocks.append((lo, rows, span, seen))
    copies = []
    for h in range(heads):
        k = 2 * (part * heads + h)
        for lo, rows, span, seen in blocks:
            q = q_ref[4 * h:4 * h + 4, lo:lo + rows].reshape(4 * rows, HD)
            s = lax.dot_general(
                q, kv_ref[k, lo:lo + span], (((1,), (1,)), ((), ())), preferred_element_type=jnp.float32
            )
            s = jnp.where(seen[None], s.reshape(4, rows, span), -jnp.inf).reshape(4 * rows, span)
            w = jnp.exp2((s - jnp.max(s, axis=1, keepdims=True)) * (scale * math.log2(math.e)))
            total = jnp.sum(w, axis=1, keepdims=True)
            o = jnp.dot(w.astype(BF), kv_ref[k + 1, lo:lo + span], preferred_element_type=jnp.float32)
            o = (o / total).astype(BF)
            for g in range(4):
                held[h, lo:lo + rows, g * HD:(g + 1) * HD] = o[g * rows:(g + 1) * rows]
        first = (part * heads + h) * 4 * HD
        cp = pltpu.make_async_copy(held.at[h], out_hbm.at[:, first:first + 4 * HD], sem.at[h])
        cp.start()
        copies.append(cp)
    for cp in copies:
        cp.wait()


def attend(part, qt, kvt, segq, segk, *prior):
    heads = TILE // 4
    whole = jax.ShapeDtypeStruct((ROWS, 2 * TILE * HD), BF)
    return pl.pallas_call(
        functools.partial(attend_kernel, part, HD ** -0.5),
        out_shape=(whole, jax.ShapeDtypeStruct((8, HD), jnp.float32)) if part == 0 else whole,
        in_specs=[VM] * 4 + [HB] * len(prior),
        out_specs=(HB, VM) if part == 0 else HB,
        scratch_shapes=[pltpu.VMEM((heads, ROWS, 4 * HD), BF), pltpu.SemaphoreType.DMA((heads,))],
        input_output_aliases={4: 0} if prior else {},
        compiler_params=params(32),
        cost_estimate=pl.CostEstimate(
            flops=4 * ROWS * 576 * TILE * HD, bytes_accessed=4 << 20, transcendentals=ROWS * 576 * TILE
        ),
        name="attend",
    )(qt, kvt, segq, segk, *prior)


def on_device(queries, key_value, route_group, arrive_slot, segment_ids):
    z, y, s = lax.axis_index("z"), lax.axis_index("y"), lax.axis_index("seq")
    kv = key_value.reshape(ROWS, TILE, HD)
    up = lambda a, n: lax.ppermute(a, "seq", [(i, i + n) for i in range(NS - n)])
    side = lambda a, n: lax.ppermute(a, "y", [(i, (i + n) % NY) for i in range(NY)])

    src, rank = arrive_slot // 6, arrive_slot % 6
    sy, sz = src & (NY - 1), src >> 2
    over = rank >= PER
    dy = (y - sy) & (NY - 1)
    idx1 = jnp.where(over, 0, (dy * NZ + sz) * PER + rank)
    idx2 = jnp.where(over, 0, sz * SLOT + dy * PER + rank)
    idx3 = jnp.where(over, 0, (sz * NY + dy) * PER + rank)

    place = jnp.arange(ROWS, dtype=jnp.int32)
    pos = jnp.stack([jnp.sum(jnp.where(rank == PER + e, place, 0)) for e in range(3)])
    note = jnp.concatenate([segment_ids.reshape(ROWS), pos])
    note1, note2 = up(note, 1), up(note, 2)

    zs1, tile, meta = pack_kv(y.reshape(1), route_group, kv, queries)
    k6 = (meta[0] - (z * NY + y)) & (NZ * NY - 1)
    dz = (((y + k6) >> 2) & (NZ - 1)).reshape(1)
    zr1 = lax.all_to_all(zs1.reshape(NZ, SLOT, TILE, HD), "z", 0, 0, tiled=True)

    tile, queries = lax.optimization_barrier((tile, queries))
    qy = pack_q(tile, queries.reshape(ROWS, 2 * TILE, HD))
    n = NZ * PER
    qy = [qy[:n]] + [side(qy[k * n:(k + 1) * n], k) for k in range(1, NY)]
    qy, note1, note2 = lax.optimization_barrier((qy, note1, note2))

    zr2 = lax.all_to_all(assemble_a(dz, qy, zr1), "z", 0, 0, tiled=True)
    zs3 = assemble_b(qy)

    part = [zr1[:, k * PER:(k + 1) * PER].reshape(NZ * PER, TILE, HD) for k in range(NY)]
    own = unpack_kv(idx1, [part[0]] + [side(part[k], k) for k in range(1, NY)])
    own2 = up(own, 2)
    own1a = lax.ppermute(own, "seq", [(i, i + 1) for i in range(0, NS, 2)])
    zs3, own2, own1a = lax.optimization_barrier((zs3, own2, own1a))
    own1b = lax.ppermute(own2, "seq", [(i + 1, i) for i in range(0, NS, 2)])
    zr3 = lax.all_to_all(zs3, "z", 0, 0, tiled=True)

    came = zr2[:EXT, SLOT - 1]
    ext = jnp.stack([came] + [side(came, k) for k in range(1, NY)])
    ext = lax.dynamic_index_in_dim(ext, k6 & (NY - 1), 0, False)
    ext0 = ext.reshape(3, 3, TILE, HD)[:, 0]
    rows, segk = window(
        s.reshape(1), (note2, note1, note), (own2, own1a, own1b, own), (up(ext0, 2), up(ext0, 1), ext0)
    )
    kvt, segq = rows.transpose(1, 0, 2), segment_ids.reshape(ROWS, 1)
    out, done = attend(0, unpack_q(1, idx2, note, zr2, ext).transpose(1, 0, 2), kvt, segq, segk)
    return attend(1, unpack_q(2, idx3, note, zr3, ext, done).transpose(1, 0, 2), kvt, segq, segk, out)


def solution(mesh):
    fine = Mesh(mesh.devices.reshape(NZ, NY, NS), ("z", "y", "seq"))
    rows = ("z", "y", "seq")
    return jax.shard_map(
        on_device,
        mesh=fine,
        in_specs=(
            P(rows, None),
            P(rows, None, None, None),
            P(rows),
            P(rows),
            P(("z", "y"), "seq"),
        ),
        out_specs=P(rows, None),
        check_vma=False,
    )
```

```python
import functools
import math

import jax
import jax.numpy as jnp
from jax import lax
from jax.experimental import pallas as pl
from jax.experimental.pallas import tpu as pltpu
from jax.sharding import Mesh, PartitionSpec as P

ROWS = 192
NZ, NY, NS = 16, 4, 8
PER = 3
TILE = 16
HD = 128
SLOT = NY * PER + 1
EXT = 9
BF = jnp.bfloat16
MIB = 1024 * 1024

VM = pl.BlockSpec(memory_space=pltpu.VMEM)
SM = pl.BlockSpec(memory_space=pltpu.SMEM)
HB = pl.BlockSpec(memory_space=pltpu.HBM)


def params(mib=16):
    return pltpu.CompilerParams(vmem_limit_bytes=mib * MIB)


def pack_kv_kernel(me_ref, rg_hbm, kv_hbm, q_hbm, out_ref, tile_ref, meta_ref, rg, nxt, xrow, kvs, qs, sem):
    plan = pltpu.make_async_copy(rg_hbm, rg, sem.at[0])
    plan.start()
    load = pltpu.make_async_copy(kv_hbm, kvs, sem.at[1])
    load.start()
    load_q = pltpu.make_async_copy(q_hbm, qs, sem.at[2])
    load_q.start()
    y = me_ref[0]
    for d in range(NZ * NY):
        nxt[d] = (d // NY * SLOT + ((d % NY - y) & (NY - 1)) * PER) * 8
    for e in range(4):
        xrow[e] = 0
    out_ref[...] = jnp.zeros_like(out_ref)
    plan.wait()

    def step(i, far):
        d = rg[i]
        n = nxt[d]
        r = n & 7
        nxt[d] = n + 9
        over = r >= PER
        tile_ref[i] = jnp.where(over, (r - PER) * 3 * SLOT + SLOT - 1, n >> 3)
        xrow[jnp.where(over, r - PER, 3)] = i
        return jnp.where(over, d, far)

    meta_ref[0] = lax.fori_loop(0, ROWS, step, 0, unroll=16)
    load.wait()

    def move(i, carry):
        out_ref[tile_ref[i]] = kvs[i]
        return carry

    lax.fori_loop(0, ROWS, move, 0, unroll=16)
    load_q.wait()
    row = lax.broadcasted_iota(jnp.int32, (16, 2 * TILE * HD), 0)
    for e in range(3):
        first = pl.multiple_of((xrow[e] >> 4) << 4, 16)
        block = qs[pl.ds(first, 16), :].astype(jnp.float32)
        one = jnp.sum(jnp.where(row == (xrow[e] & 15), block, 0.0), axis=0, keepdims=True)
        for t in range(2):
            parts = [one[:, (t * TILE + c) * HD:(t * TILE + c + 1) * HD] for c in range(TILE)]
            out_ref[(e * 3 + 1 + t) * SLOT + SLOT - 1] = jnp.concatenate(parts, axis=0).astype(BF)


def pack_kv(me, rg, kv, q):
    return pl.pallas_call(
        pack_kv_kernel,
        out_shape=(
            jax.ShapeDtypeStruct((NZ * SLOT, TILE, HD), BF),
            jax.ShapeDtypeStruct((ROWS,), jnp.int32),
            jax.ShapeDtypeStruct((1,), jnp.int32),
        ),
        in_specs=[SM, HB, HB, HB],
        out_specs=(VM, SM, SM),
        scratch_shapes=[
            pltpu.SMEM((ROWS,), jnp.int32),
            pltpu.SMEM((NZ * NY,), jnp.int32),
            pltpu.SMEM((4,), jnp.int32),
            pltpu.VMEM((ROWS, TILE, HD), BF),
            pltpu.VMEM((ROWS, 2 * TILE * HD), BF),
            pltpu.SemaphoreType.DMA((3,)),
        ],
        compiler_params=params(60),
        name="pack_kv",
    )(me, rg, kv, q)


def pack_q_kernel(tile_ref, q_ref, out_ref):
    out_ref[...] = jnp.zeros_like(out_ref)

    def step(i, carry):
        t = tile_ref[i]
        gz = (t * 79) >> 10
        k = t - gz * SLOT
        dy = (k * 11) >> 5
        out_ref[jnp.where(k == SLOT - 1, ROWS, (dy * NZ + gz) * PER + k - dy * PER)] = q_ref[i]
        return carry

    lax.fori_loop(0, ROWS, step, 0, unroll=16)


def pack_q(tile, q3):
    return pl.pallas_call(
        pack_q_kernel,
        out_shape=jax.ShapeDtypeStruct((ROWS + 1, 2 * TILE, HD), BF),
        in_specs=[SM, VM],
        out_specs=VM,
        compiler_params=params(),
        name="pack_q",
    )(tile, q3)


def assemble_kernel(b0, b1, b2, b3, a_ref, b_ref):
    for z in range(NZ):
        for k, b in enumerate((b0, b1, b2, b3)):
            rows = b[z * PER:(z + 1) * PER]
            a_ref[z, k * PER:(k + 1) * PER] = rows[:, :TILE]
            b_ref[z, k * PER:(k + 1) * PER] = rows[:, TILE:]
        a_ref[z, SLOT - 1] = jnp.zeros((TILE, HD), BF)


def assemble(blocks):
    return pl.pallas_call(
        assemble_kernel,
        out_shape=(
            jax.ShapeDtypeStruct((NZ, SLOT, TILE, HD), BF),
            jax.ShapeDtypeStruct((NZ, NY * PER, TILE, HD), BF),
        ),
        in_specs=[VM] * NY,
        out_specs=(VM, VM),
        compiler_params=params(),
        name="assemble",
    )(*blocks)


def hop_kernel(dz_ref, _, came, out, sem):
    copies = []
    for z in range(NZ):
        cp = pltpu.make_async_copy(
            came.at[(z - dz_ref[0]) & (NZ - 1), SLOT - 1], out.at[z, SLOT - 1], sem.at[z]
        )
        cp.start()
        copies.append(cp)
    for cp in copies:
        cp.wait()


def hop(dz, zs, came):
    return pl.pallas_call(
        hop_kernel,
        out_shape=jax.ShapeDtypeStruct(zs.shape, zs.dtype),
        in_specs=[SM, HB, HB],
        out_specs=HB,
        scratch_shapes=[pltpu.SemaphoreType.DMA((NZ,))],
        input_output_aliases={1: 0},
        compiler_params=params(),
        name="hop",
    )(dz, zs, came)


def unpack_kv_kernel(idx_ref, b0, b1, b2, b3, out_ref, held):
    for k, b in enumerate((b0, b1, b2, b3)):
        held[k * NZ * PER:(k + 1) * NZ * PER] = b[...]

    def step(p, carry):
        out_ref[p] = held[idx_ref[p]]
        return carry

    lax.fori_loop(0, ROWS, step, 0, unroll=8)


def unpack_kv(idx, blocks):
    return pl.pallas_call(
        unpack_kv_kernel,
        out_shape=jax.ShapeDtypeStruct((ROWS, TILE, HD), BF),
        in_specs=[SM] + [VM] * NY,
        out_specs=VM,
        scratch_shapes=[pltpu.VMEM((ROWS, TILE, HD), BF)],
        compiler_params=params(),
        name="unpack_kv",
    )(idx, *blocks)


def window_kernel(at_ref, n2, n1, n0, m2, m1, m0, h2, h1a, h1b, h0, e2, e1, e0, out_ref, seg_ref):
    out_ref[:ROWS] = h2[...]
    out_ref[ROWS:2 * ROWS] = h1a[...] + h1b[...]
    out_ref[2 * ROWS:] = h0[...]
    for k, (n, e) in enumerate(((n2, e2), (n1, e1), (n0, e0))):
        for i in range(3):
            out_ref[k * ROWS + n[ROWS + i]] = e[i]
    at = at_ref[0]
    seg_ref[:, :ROWS] = jnp.where(at >= 2, m2[:, :ROWS], -1)
    seg_ref[:, ROWS:2 * ROWS] = jnp.where(at >= 1, m1[:, :ROWS], -1)
    seg_ref[:, 2 * ROWS:] = m0[:, :ROWS]


def window(at, notes, rows, extra):
    return pl.pallas_call(
        window_kernel,
        out_shape=(
            jax.ShapeDtypeStruct((3 * ROWS, TILE, HD), BF),
            jax.ShapeDtypeStruct((1, 3 * ROWS), jnp.int32),
        ),
        in_specs=[SM] * 4 + [VM] * 10,
        out_specs=(VM, VM),
        compiler_params=params(),
        name="window",
    )(at, *notes, *[n[None] for n in notes], *rows, *extra)


def unpack_q_kernel(part, idx_ref, note_ref, src_ref, ext_ref, *rest):
    out_ref = rest[-1]

    def step(p, carry):
        out_ref[p] = src_ref[idx_ref[p]]
        return carry

    lax.fori_loop(0, ROWS, step, 0, unroll=16)
    for e in range(3):
        out_ref[note_ref[ROWS + e]] = ext_ref[e * 3 + part]


def unpack_q(part, idx, note, zr, ext, *after):
    return pl.pallas_call(
        functools.partial(unpack_q_kernel, part),
        out_shape=jax.ShapeDtypeStruct((ROWS, TILE, HD), BF),
        in_specs=[SM, SM, VM, VM] + [VM] * len(after),
        out_specs=VM,
        compiler_params=params(),
        name="unpack_q",
    )(idx, note, zr.reshape(-1, TILE, HD), ext, *after)


def attend_kernel(part, scale, q_ref, kv_ref, segq_ref, segk_ref, *rest):
    if part == 0:
        out_hbm, done_ref, held, sem = rest
        done_ref[...] = jnp.zeros_like(done_ref)
    else:
        _, out_hbm, held, sem = rest
    heads = TILE // 4
    blocks = []
    for lo, rows in ((0, 128), (128, 64)):
        span = min(rows + 2 * ROWS, 3 * ROWS - lo)
        i = lax.broadcasted_iota(jnp.int32, (rows, span), 0)
        j = lax.broadcasted_iota(jnp.int32, (rows, span), 1)
        seen = (segq_ref[lo:lo + rows, :] == segk_ref[:, lo:lo + span]) & (j <= i + 2 * ROWS)
        blocks.append((lo, rows, span, seen))
    units = [(h, b) for h in range(heads) for b in range(len(blocks))]

    def scores(h, b):
        lo, rows, span, _ = blocks[b]
        q = q_ref[4 * h:4 * h + 4, lo:lo + rows].reshape(4 * rows, HD)
        keys = kv_ref[2 * (part * heads + h), lo:lo + span]
        return lax.dot_general(q, keys, (((1,), (1,)), ((), ())), preferred_element_type=jnp.float32)

    copies = []
    later = scores(*units[0])
    for n, (h, b) in enumerate(units):
        lo, rows, span, seen = blocks[b]
        s = later
        if n + 1 < len(units):
            later = scores(*units[n + 1])
        s = jnp.where(seen[None], s.reshape(4, rows, span), -jnp.inf).reshape(4 * rows, span)
        w = jnp.exp2((s - jnp.max(s, axis=1, keepdims=True)) * (scale * math.log2(math.e)))
        total = jnp.sum(w, axis=1, keepdims=True)
        values = kv_ref[2 * (part * heads + h) + 1, lo:lo + span]
        o = jnp.dot(w.astype(BF), values, preferred_element_type=jnp.float32)
        o = (o / total).astype(BF)
        for g in range(4):
            held[h, lo:lo + rows, g * HD:(g + 1) * HD] = o[g * rows:(g + 1) * rows]
        if b == len(blocks) - 1:
            first = (part * heads + h) * 4 * HD
            cp = pltpu.make_async_copy(held.at[h], out_hbm.at[:, first:first + 4 * HD], sem.at[h])
            cp.start()
            copies.append(cp)
    for cp in copies:
        cp.wait()


def attend(part, qt, kvt, segq, segk, *prior):
    heads = TILE // 4
    whole = jax.ShapeDtypeStruct((ROWS, 2 * TILE * HD), BF)
    return pl.pallas_call(
        functools.partial(attend_kernel, part, HD ** -0.5),
        out_shape=(whole, jax.ShapeDtypeStruct((8, HD), jnp.float32)) if part == 0 else whole,
        in_specs=[VM] * 4 + [HB] * len(prior),
        out_specs=(HB, VM) if part == 0 else HB,
        scratch_shapes=[pltpu.VMEM((heads, ROWS, 4 * HD), BF), pltpu.SemaphoreType.DMA((heads,))],
        input_output_aliases={4: 0} if prior else {},
        compiler_params=params(32),
        cost_estimate=pl.CostEstimate(
            flops=4 * ROWS * 576 * TILE * HD, bytes_accessed=4 << 20, transcendentals=ROWS * 576 * TILE
        ),
        name="attend",
    )(qt, kvt, segq, segk, *prior)


def on_device(queries, key_value, route_group, arrive_slot, segment_ids):
    z, y, s = lax.axis_index("z"), lax.axis_index("y"), lax.axis_index("seq")
    kv = key_value.reshape(ROWS, TILE, HD)
    up = lambda a, n: lax.ppermute(a, "seq", [(i, i + n) for i in range(NS - n)])
    side = lambda a, n: lax.ppermute(a, "y", [(i, (i + n) % NY) for i in range(NY)])

    src, rank = arrive_slot // 6, arrive_slot % 6
    sy, sz = src & (NY - 1), src >> 2
    over = rank >= PER
    dy = (y - sy) & (NY - 1)
    idx1 = jnp.where(over, 0, (dy * NZ + sz) * PER + rank)
    idx2 = jnp.where(over, 0, sz * SLOT + dy * PER + rank)
    idx3 = jnp.where(over, 0, (sz * NY + dy) * PER + rank)

    place = jnp.arange(ROWS, dtype=jnp.int32)
    pos = jnp.stack([jnp.sum(jnp.where(rank == PER + e, place, 0)) for e in range(3)])
    note = jnp.concatenate([segment_ids.reshape(ROWS), pos])
    note1, note2 = up(note, 1), up(note, 2)

    zs1, tile, meta = pack_kv(y.reshape(1), route_group, kv, queries)
    k6 = (meta[0] - (z * NY + y)) & (NZ * NY - 1)
    dz = (((y + k6) >> 2) & (NZ - 1)).reshape(1)
    zr1 = lax.all_to_all(zs1.reshape(NZ, SLOT, TILE, HD), "z", 0, 0, tiled=True)

    tile, queries = lax.optimization_barrier((tile, queries))
    qy = pack_q(tile, queries.reshape(ROWS, 2 * TILE, HD))
    n = NZ * PER
    qy = [qy[:n]] + [side(qy[k * n:(k + 1) * n], k) for k in range(1, NY)]
    zs2, zs3 = assemble(qy)
    zs2, zs3, note1, note2, dz = lax.optimization_barrier((zs2, zs3, note1, note2, dz))
    zr2 = lax.all_to_all(hop(dz, zs2, zr1), "z", 0, 0, tiled=True)

    part = [zr1[:, k * PER:(k + 1) * PER].reshape(NZ * PER, TILE, HD) for k in range(NY)]
    own = unpack_kv(idx1, [part[0]] + [side(part[k], k) for k in range(1, NY)])
    own2 = up(own, 2)
    own1a = lax.ppermute(own, "seq", [(i, i + 1) for i in range(0, NS, 2)])
    zs3, own2, own1a = lax.optimization_barrier((zs3, own2, own1a))
    own1b = lax.ppermute(own2, "seq", [(i + 1, i) for i in range(0, NS, 2)])
    zr3 = lax.all_to_all(zs3, "z", 0, 0, tiled=True)

    came = zr2[:EXT, SLOT - 1]
    ext = jnp.stack([came] + [side(came, k) for k in range(1, NY)])
    ext = lax.dynamic_index_in_dim(ext, k6 & (NY - 1), 0, False)
    ext0 = ext.reshape(3, 3, TILE, HD)[:, 0]
    rows, segk = window(
        s.reshape(1), (note2, note1, note), (own2, own1a, own1b, own), (up(ext0, 2), up(ext0, 1), ext0)
    )
    kvt, segq = rows.transpose(1, 0, 2), segment_ids.reshape(ROWS, 1)
    out, done = attend(0, unpack_q(1, idx2, note, zr2, ext).transpose(1, 0, 2), kvt, segq, segk)
    return attend(1, unpack_q(2, idx3, note, zr3, ext, done).transpose(1, 0, 2), kvt, segq, segk, out)


def solution(mesh):
    fine = Mesh(mesh.devices.reshape(NZ, NY, NS), ("z", "y", "seq"))
    rows = ("z", "y", "seq")
    return jax.shard_map(
        on_device,
        mesh=fine,
        in_specs=(
            P(rows, None),
            P(rows, None, None, None),
            P(rows),
            P(rows),
            P(("z", "y"), "seq"),
        ),
        out_specs=P(rows, None),
        check_vma=False,
    )
```

```python
import functools
import math

import jax
import jax.numpy as jnp
from jax import lax
from jax.experimental import pallas as pl
from jax.experimental.pallas import tpu as pltpu
from jax.sharding import Mesh, PartitionSpec as P

ROWS = 192
NZ, NY, NS = 16, 4, 8
PER = 3
HD = 128
UNIT = 4
KV, QA, QB = 4, 5, 3
BASE = NY * PER
HOP = 3
EXT = 3 * (KV + QA + QB)
SLOT1, SLOT2, SLOT3 = BASE * KV + HOP, BASE * QA + HOP, BASE * QB
BF = jnp.bfloat16
MIB = 1024 * 1024

VM = pl.BlockSpec(memory_space=pltpu.VMEM)
SM = pl.BlockSpec(memory_space=pltpu.SMEM)
HB = pl.BlockSpec(memory_space=pltpu.HBM)


def params(mib=16):
    return pltpu.CompilerParams(vmem_limit_bytes=mib * MIB)


def pack_kv_kernel(me_ref, rg_hbm, kv_hbm, q_hbm, out_hbm, tile_ref, meta_ref, rg, nxt, xrow, kvs, qs, held, sem):
    plan = pltpu.make_async_copy(rg_hbm, rg, sem.at[0])
    plan.start()
    load = pltpu.make_async_copy(kv_hbm, kvs, sem.at[1])
    load.start()
    load_q = pltpu.make_async_copy(q_hbm, qs, sem.at[2])
    load_q.start()
    y = me_ref[0]
    for d in range(NZ * NY):
        nxt[d] = (d // NY * SLOT1 + ((d % NY - y) & (NY - 1)) * PER * KV) * 8
    for e in range(4):
        xrow[e] = 0
    held[...] = jnp.zeros_like(held)
    plan.wait()

    def step(i, far):
        d = rg[i]
        n = nxt[d]
        r = n & 7
        nxt[d] = n + KV * 8 + 1
        over = r >= PER
        tile_ref[i] = jnp.where(over, NZ * SLOT1, n >> 3)
        xrow[jnp.where(over, r - PER, 3)] = i
        return jnp.where(over, d, far)

    meta_ref[0] = lax.fori_loop(0, ROWS, step, 0, unroll=16)
    load.wait()

    def move(i, carry):
        held[pl.ds(tile_ref[i], KV)] = kvs[i]
        return carry

    lax.fori_loop(0, ROWS, move, 0, unroll=16)
    load_q.wait()
    row = lax.broadcasted_iota(jnp.int32, (16, (QA + QB) * UNIT * HD), 0)

    def place(e, u):
        j = e * (KV + QA + QB) + u
        return j // HOP * SLOT1 + BASE * KV + j % HOP

    for e in range(3):
        for u in range(KV):
            held[place(e, u)] = kvs[xrow[e], u]
        first = pl.multiple_of((xrow[e] >> 4) << 4, 16)
        block = qs[pl.ds(first, 16), :].astype(jnp.float32)
        one = jnp.sum(jnp.where(row == (xrow[e] & 15), block, 0.0), axis=0, keepdims=True)
        for u in range(QA + QB):
            parts = [one[:, (u * UNIT + c) * HD:(u * UNIT + c + 1) * HD] for c in range(UNIT)]
            held[place(e, KV + u)] = jnp.concatenate(parts, axis=0).astype(BF)
    store = pltpu.make_async_copy(held.at[pl.ds(0, NZ * SLOT1)], out_hbm, sem.at[3])
    store.start()
    store.wait()


def pack_kv(me, rg, kv, q):
    return pl.pallas_call(
        pack_kv_kernel,
        out_shape=(
            jax.ShapeDtypeStruct((NZ * SLOT1, UNIT, HD), BF),
            jax.ShapeDtypeStruct((ROWS,), jnp.int32),
            jax.ShapeDtypeStruct((1,), jnp.int32),
        ),
        in_specs=[SM, HB, HB, HB],
        out_specs=(HB, SM, SM),
        scratch_shapes=[
            pltpu.SMEM((ROWS,), jnp.int32),
            pltpu.SMEM((NZ * NY,), jnp.int32),
            pltpu.SMEM((4,), jnp.int32),
            pltpu.VMEM((ROWS, KV, UNIT, HD), BF),
            pltpu.VMEM((ROWS, (QA + QB) * UNIT * HD), BF),
            pltpu.VMEM((NZ * SLOT1 + KV, UNIT, HD), BF),
            pltpu.SemaphoreType.DMA((4,)),
        ],
        compiler_params=params(60),
        name="pack_kv",
    )(me, rg, kv, q)


def pack_q_kernel(tile_ref, q_ref, out_ref):
    out_ref[...] = jnp.zeros_like(out_ref)

    def step(i, carry):
        t = tile_ref[i]
        gz = (t * 1286) >> 16
        k = (t - gz * SLOT1) >> 2
        dy = (k * 11) >> 5
        out_ref[jnp.where(gz == NZ, ROWS, (dy * NZ + gz) * PER + k - dy * PER)] = q_ref[i]
        return carry

    lax.fori_loop(0, ROWS, step, 0, unroll=16)


def pack_q(tile, q):
    return pl.pallas_call(
        pack_q_kernel,
        out_shape=jax.ShapeDtypeStruct((ROWS + 1, QA + QB, UNIT, HD), BF),
        in_specs=[SM, VM],
        out_specs=VM,
        compiler_params=params(),
        name="pack_q",
    )(tile, q)


def assemble_kernel(b0, b1, b2, b3, a_ref, b_ref):
    for k, b in enumerate((b0, b1, b2, b3)):

        def step(z, carry, k=k, b=b):
            for r in range(PER):
                a_ref[z, (k * PER + r) * QA:(k * PER + r + 1) * QA] = b[z * PER + r, :QA]
                b_ref[z, (k * PER + r) * QB:(k * PER + r + 1) * QB] = b[z * PER + r, QA:]
            return carry

        lax.fori_loop(0, NZ, step, 0, unroll=4)
    a_ref[:, SLOT2 - HOP:] = jnp.zeros((NZ, HOP, UNIT, HD), BF)


def assemble(blocks):
    return pl.pallas_call(
        assemble_kernel,
        out_shape=(
            jax.ShapeDtypeStruct((NZ, SLOT2, UNIT, HD), BF),
            jax.ShapeDtypeStruct((NZ, SLOT3, UNIT, HD), BF),
        ),
        in_specs=[VM] * NY,
        out_specs=(VM, VM),
        compiler_params=params(),
        name="assemble",
    )(*blocks)


def hop_kernel(dz_ref, _, came, out, sem):
    copies = []
    for z in range(NZ):
        cp = pltpu.make_async_copy(
            came.at[(z - dz_ref[0]) & (NZ - 1), pl.ds(SLOT1 - HOP, HOP)],
            out.at[z, pl.ds(SLOT2 - HOP, HOP)],
            sem.at[z],
        )
        cp.start()
        copies.append(cp)
    for cp in copies:
        cp.wait()


def hop(dz, zs, came):
    return pl.pallas_call(
        hop_kernel,
        out_shape=jax.ShapeDtypeStruct(zs.shape, zs.dtype),
        in_specs=[SM, HB, HB],
        out_specs=HB,
        scratch_shapes=[pltpu.SemaphoreType.DMA((NZ,))],
        input_output_aliases={1: 0},
        compiler_params=params(),
        name="hop",
    )(dz, zs, came)


def unpack_kv_kernel(idx_ref, b0, b1, b2, b3, out_ref, held):
    for k, b in enumerate((b0, b1, b2, b3)):
        held[k * NZ * PER:(k + 1) * NZ * PER] = b[...]

    def step(p, carry):
        out_ref[p] = held[idx_ref[p]]
        return carry

    lax.fori_loop(0, ROWS, step, 0, unroll=8)


def unpack_kv(idx, blocks):
    return pl.pallas_call(
        unpack_kv_kernel,
        out_shape=jax.ShapeDtypeStruct((ROWS, KV, UNIT, HD), BF),
        in_specs=[SM] + [VM] * NY,
        out_specs=VM,
        scratch_shapes=[pltpu.VMEM((ROWS, KV, UNIT, HD), BF)],
        compiler_params=params(),
        name="unpack_kv",
    )(idx, *blocks)


def window_kernel(at_ref, n2, n1, n0, m2, m1, m0, h2, h1a, h1b, h0, e2, e1, e0, out_ref, seg_ref):
    out_ref[:ROWS] = h2[...]
    out_ref[ROWS:2 * ROWS] = h1a[...] + h1b[...]
    out_ref[2 * ROWS:] = h0[...]
    for k, (n, e) in enumerate(((n2, e2), (n1, e1), (n0, e0))):
        for i in range(3):
            out_ref[k * ROWS + n[ROWS + i]] = e[i]
    at = at_ref[0]
    seg_ref[:, :ROWS] = jnp.where(at >= 2, m2[:, :ROWS], -1)
    seg_ref[:, ROWS:2 * ROWS] = jnp.where(at >= 1, m1[:, :ROWS], -1)
    seg_ref[:, 2 * ROWS:] = m0[:, :ROWS]


def window(at, notes, rows, extra):
    wide = lambda a: a.reshape(-1, KV * UNIT, HD)
    return pl.pallas_call(
        window_kernel,
        out_shape=(
            jax.ShapeDtypeStruct((3 * ROWS, KV * UNIT, HD), BF),
            jax.ShapeDtypeStruct((1, 3 * ROWS), jnp.int32),
        ),
        in_specs=[SM] * 4 + [VM] * 10,
        out_specs=(VM, VM),
        compiler_params=params(),
        name="window",
    )(at, *notes, *[n[None] for n in notes], *map(wide, rows), *map(wide, extra))


def unpack_q_kernel(first, units, idx_ref, note_ref, src_ref, ext_ref, *rest):
    out_ref = rest[-1]

    def step(p, carry):
        out_ref[p] = src_ref[pl.ds(idx_ref[p], units)]
        return carry

    lax.fori_loop(0, ROWS, step, 0, unroll=16)
    for e in range(3):
        out_ref[note_ref[ROWS + e]] = ext_ref[e, first:first + units]


def unpack_q(first, units, idx, note, zr, ext, *after):
    rows = pl.pallas_call(
        functools.partial(unpack_q_kernel, first, units),
        out_shape=jax.ShapeDtypeStruct((ROWS, units, UNIT, HD), BF),
        in_specs=[SM, SM, VM, VM] + [VM] * len(after),
        out_specs=VM,
        compiler_params=params(),
        name="unpack_q",
    )(idx, note, zr.reshape(-1, UNIT, HD), ext, *after)
    return rows.reshape(ROWS, units * UNIT, HD).transpose(1, 0, 2)


def attend_kernel(part, heads, scale, q_ref, kv_ref, segq_ref, segk_ref, *rest):
    if part == 0:
        out_hbm, done_ref, held, sem = rest
        done_ref[...] = jnp.zeros_like(done_ref)
    else:
        _, out_hbm, held, sem = rest
    base = part * QA
    blocks = []
    for lo, rows in ((0, 128), (128, 64)):
        span = min(rows + 2 * ROWS, 3 * ROWS - lo)
        i = lax.broadcasted_iota(jnp.int32, (rows, span), 0)
        j = lax.broadcasted_iota(jnp.int32, (rows, span), 1)
        seen = (segq_ref[lo:lo + rows, :] == segk_ref[:, lo:lo + span]) & (j <= i + 2 * ROWS)
        blocks.append((lo, rows, span, seen))
    units = [(h, b) for h in range(heads) for b in range(len(blocks))]

    def scores(h, b):
        lo, rows, span, _ = blocks[b]
        q = q_ref[4 * h:4 * h + 4, lo:lo + rows].reshape(4 * rows, HD)
        keys = kv_ref[2 * (base + h), lo:lo + span]
        return lax.dot_general(q, keys, (((1,), (1,)), ((), ())), preferred_element_type=jnp.float32)

    copies = []
    later = scores(*units[0])
    for n, (h, b) in enumerate(units):
        lo, rows, span, seen = blocks[b]
        s = later
        if n + 1 < len(units):
            later = scores(*units[n + 1])
        s = jnp.where(seen[None], s.reshape(4, rows, span), -jnp.inf).reshape(4 * rows, span)
        w = jnp.exp2((s - jnp.max(s, axis=1, keepdims=True)) * (scale * math.log2(math.e)))
        total = jnp.sum(w, axis=1, keepdims=True)
        values = kv_ref[2 * (base + h) + 1, lo:lo + span]
        o = jnp.dot(w.astype(BF), values, preferred_element_type=jnp.float32)
        o = (o / total).astype(BF)
        for g in range(4):
            held[h, lo:lo + rows, g * HD:(g + 1) * HD] = o[g * rows:(g + 1) * rows]
        if b == len(blocks) - 1:
            first = (base + h) * 4 * HD
            cp = pltpu.make_async_copy(held.at[h], out_hbm.at[:, first:first + 4 * HD], sem.at[h])
            cp.start()
            copies.append(cp)
    for cp in copies:
        cp.wait()


def attend(part, qt, kvt, segq, segk, *prior):
    heads = QB if part else QA
    whole = jax.ShapeDtypeStruct((ROWS, (QA + QB) * UNIT * HD), BF)
    return pl.pallas_call(
        functools.partial(attend_kernel, part, heads, HD ** -0.5),
        out_shape=(whole, jax.ShapeDtypeStruct((8, HD), jnp.float32)) if part == 0 else whole,
        in_specs=[VM] * 4 + [HB] * len(prior),
        out_specs=(HB, VM) if part == 0 else HB,
        scratch_shapes=[pltpu.VMEM((heads, ROWS, 4 * HD), BF), pltpu.SemaphoreType.DMA((heads,))],
        input_output_aliases={4: 0} if prior else {},
        compiler_params=params(32),
        cost_estimate=pl.CostEstimate(
            flops=16 * ROWS * 576 * heads * HD, bytes_accessed=4 << 20, transcendentals=4 * ROWS * 576 * heads
        ),
        name="attend",
    )(qt, kvt, segq, segk, *prior)


def on_device(queries, key_value, route_group, arrive_slot, segment_ids):
    z, y, s = lax.axis_index("z"), lax.axis_index("y"), lax.axis_index("seq")
    kv = key_value.reshape(ROWS, KV, UNIT, HD)
    up = lambda a, n: lax.ppermute(a, "seq", [(i, i + n) for i in range(NS - n)])
    side = lambda a, n: lax.ppermute(a, "y", [(i, (i + n) % NY) for i in range(NY)])

    src, rank = arrive_slot // 6, arrive_slot % 6
    sy, sz = src & (NY - 1), src >> 2
    over = rank >= PER
    dy = (y - sy) & (NY - 1)
    idx1 = jnp.where(over, 0, (dy * NZ + sz) * PER + rank)
    idx2 = jnp.where(over, 0, sz * SLOT2 + (dy * PER + rank) * QA)
    idx3 = jnp.where(over, 0, sz * SLOT3 + (dy * PER + rank) * QB)

    place = jnp.arange(ROWS, dtype=jnp.int32)
    pos = jnp.stack([jnp.sum(jnp.where(rank == PER + e, place, 0)) for e in range(3)])
    note = jnp.concatenate([segment_ids.reshape(ROWS), pos])
    note1, note2 = up(note, 1), up(note, 2)

    zs1, tile, meta = pack_kv(y.reshape(1), route_group, kv, queries)
    k6 = (meta[0] - (z * NY + y)) & (NZ * NY - 1)
    dz = (((y + k6) >> 2) & (NZ - 1)).reshape(1)
    zr1 = lax.all_to_all(zs1.reshape(NZ, SLOT1, UNIT, HD), "z", 0, 0, tiled=True)

    tile, queries = lax.optimization_barrier((tile, queries))
    qy = pack_q(tile, queries.reshape(ROWS, QA + QB, UNIT, HD))
    n = NZ * PER
    qy = [qy[:n]] + [side(qy[k * n:(k + 1) * n], k) for k in range(1, NY)]
    zs2, zs3 = assemble(qy)
    zs2, zs3, note1, note2, dz = lax.optimization_barrier((zs2, zs3, note1, note2, dz))
    zr2 = lax.all_to_all(hop(dz, zs2, zr1), "z", 0, 0, tiled=True)

    run = PER * KV
    part = [zr1[:, k * run:(k + 1) * run].reshape(NZ * PER, KV, UNIT, HD) for k in range(NY)]
    own = unpack_kv(idx1, [part[0]] + [side(part[k], k) for k in range(1, NY)])
    own2 = up(own, 2)
    own1a = lax.ppermute(own, "seq", [(i, i + 1) for i in range(0, NS, 2)])
    zs3, own2, own1a = lax.optimization_barrier((zs3, own2, own1a))
    own1b = lax.ppermute(own2, "seq", [(i + 1, i) for i in range(0, NS, 2)])
    zr3 = lax.all_to_all(zs3, "z", 0, 0, tiled=True)

    came = zr2[:EXT // HOP, SLOT2 - HOP:].reshape(EXT, UNIT, HD)
    ext = jnp.stack([came] + [side(came, k) for k in range(1, NY)])
    ext = lax.dynamic_index_in_dim(ext, k6 & (NY - 1), 0, False).reshape(3, EXT // 3, UNIT, HD)
    ext0 = ext[:, :KV]
    rows, segk = window(
        s.reshape(1), (note2, note1, note), (own2, own1a, own1b, own), (up(ext0, 2), up(ext0, 1), ext0)
    )
    kvt, segq = rows.transpose(1, 0, 2), segment_ids.reshape(ROWS, 1)
    out, done = attend(0, unpack_q(KV, QA, idx2, note, zr2, ext), kvt, segq, segk)
    return attend(1, unpack_q(KV + QA, QB, idx3, note, zr3, ext, done), kvt, segq, segk, out)


def solution(mesh):
    fine = Mesh(mesh.devices.reshape(NZ, NY, NS), ("z", "y", "seq"))
    rows = ("z", "y", "seq")
    return jax.shard_map(
        on_device,
        mesh=fine,
        in_specs=(
            P(rows, None),
            P(rows, None, None, None),
            P(rows),
            P(rows),
            P(("z", "y"), "seq"),
        ),
        out_specs=P(rows, None),
        check_vma=False,
    )
```

```python
import functools
import math

import jax
import jax.numpy as jnp
from jax import lax
from jax.experimental import pallas as pl
from jax.experimental.pallas import tpu as pltpu
from jax.sharding import Mesh, PartitionSpec as P

ROWS = 192
NZ, NY, NS = 16, 4, 8
PER = 3
HD = 128
UNIT = 4
KV, QA, QB = 4, 5, 3
BASE = NY * PER
HOP = 3
EXT = 3 * (KV + QA + QB)
SLOT1, SLOT2, SLOT3 = BASE * KV + HOP, BASE * QA + HOP, BASE * QB
BF = jnp.bfloat16
MIB = 1024 * 1024

VM = pl.BlockSpec(memory_space=pltpu.VMEM)
SM = pl.BlockSpec(memory_space=pltpu.SMEM)
HB = pl.BlockSpec(memory_space=pltpu.HBM)


def params(mib=16):
    return pltpu.CompilerParams(vmem_limit_bytes=mib * MIB)


def pack_kv_kernel(me_ref, rg_hbm, kv_hbm, q_hbm, out_hbm, tile_ref, meta_ref, rg, nxt, xrow, kvs, qs, held, sem):
    plan = pltpu.make_async_copy(rg_hbm, rg, sem.at[0])
    plan.start()
    load = pltpu.make_async_copy(kv_hbm, kvs, sem.at[1])
    load.start()
    load_q = pltpu.make_async_copy(q_hbm, qs, sem.at[2])
    load_q.start()
    y = me_ref[0]
    for d in range(NZ * NY):
        nxt[d] = (d // NY * SLOT1 + ((d % NY - y) & (NY - 1)) * PER * KV) * 8
    for e in range(4):
        xrow[e] = 0
    plan.wait()

    def step(i, far):
        d = rg[i]
        n = nxt[d]
        r = n & 7
        nxt[d] = n + KV * 8 + 1
        over = r >= PER
        tile_ref[i] = jnp.where(over, NZ * SLOT1, n >> 3)
        xrow[jnp.where(over, r - PER, 3)] = i
        return jnp.where(over, d, far)

    meta_ref[0] = lax.fori_loop(0, ROWS, step, 0, unroll=16)
    load.wait()

    def move(i, carry):
        held[pl.ds(tile_ref[i], KV)] = kvs[i]
        return carry

    lax.fori_loop(0, ROWS, move, 0, unroll=16)
    load_q.wait()
    row = lax.broadcasted_iota(jnp.int32, (16, (QA + QB) * UNIT * HD), 0)

    def place(e, u):
        j = e * (KV + QA + QB) + u
        return j // HOP * SLOT1 + BASE * KV + j % HOP

    for e in range(3):
        for u in range(KV):
            held[place(e, u)] = kvs[xrow[e], u]
        first = pl.multiple_of((xrow[e] >> 4) << 4, 16)
        block = qs[pl.ds(first, 16), :].astype(jnp.float32)
        one = jnp.sum(jnp.where(row == (xrow[e] & 15), block, 0.0), axis=0, keepdims=True)
        for u in range(QA + QB):
            parts = [one[:, (u * UNIT + c) * HD:(u * UNIT + c + 1) * HD] for c in range(UNIT)]
            held[place(e, KV + u)] = jnp.concatenate(parts, axis=0).astype(BF)
    store = pltpu.make_async_copy(held.at[pl.ds(0, NZ * SLOT1)], out_hbm, sem.at[3])
    store.start()
    store.wait()


def pack_kv(me, rg, kv, q):
    return pl.pallas_call(
        pack_kv_kernel,
        out_shape=(
            jax.ShapeDtypeStruct((NZ * SLOT1, UNIT, HD), BF),
            jax.ShapeDtypeStruct((ROWS,), jnp.int32),
            jax.ShapeDtypeStruct((1,), jnp.int32),
        ),
        in_specs=[SM, HB, HB, HB],
        out_specs=(HB, SM, SM),
        scratch_shapes=[
            pltpu.SMEM((ROWS,), jnp.int32),
            pltpu.SMEM((NZ * NY,), jnp.int32),
            pltpu.SMEM((4,), jnp.int32),
            pltpu.VMEM((ROWS, KV, UNIT, HD), BF),
            pltpu.VMEM((ROWS, (QA + QB) * UNIT * HD), BF),
            pltpu.VMEM((NZ * SLOT1 + KV, UNIT, HD), BF),
            pltpu.SemaphoreType.DMA((4,)),
        ],
        compiler_params=params(60),
        name="pack_kv",
    )(me, rg, kv, q)


def pack_q_kernel(tile_ref, q_ref, out_ref):
    out_ref[...] = jnp.zeros_like(out_ref)

    def step(i, carry):
        t = tile_ref[i]
        gz = (t * 1286) >> 16
        k = (t - gz * SLOT1) >> 2
        dy = (k * 11) >> 5
        out_ref[jnp.where(gz == NZ, ROWS, (dy * NZ + gz) * PER + k - dy * PER)] = q_ref[i]
        return carry

    lax.fori_loop(0, ROWS, step, 0, unroll=16)


def pack_q(tile, q):
    return pl.pallas_call(
        pack_q_kernel,
        out_shape=jax.ShapeDtypeStruct((ROWS + 1, QA + QB, UNIT, HD), BF),
        in_specs=[SM, VM],
        out_specs=VM,
        compiler_params=params(),
        name="pack_q",
    )(tile, q)


def assemble_kernel(b0, b1, b2, b3, a_ref, b_ref):
    for k, b in enumerate((b0, b1, b2, b3)):

        def step(z, carry, k=k, b=b):
            for r in range(PER):
                a_ref[z, (k * PER + r) * QA:(k * PER + r + 1) * QA] = b[z * PER + r, :QA]
                b_ref[z, (k * PER + r) * QB:(k * PER + r + 1) * QB] = b[z * PER + r, QA:]
            return carry

        lax.fori_loop(0, NZ, step, 0, unroll=4)
    a_ref[:, SLOT2 - HOP:] = jnp.zeros((NZ, HOP, UNIT, HD), BF)


def assemble(blocks):
    return pl.pallas_call(
        assemble_kernel,
        out_shape=(
            jax.ShapeDtypeStruct((NZ, SLOT2, UNIT, HD), BF),
            jax.ShapeDtypeStruct((NZ, SLOT3, UNIT, HD), BF),
        ),
        in_specs=[VM] * NY,
        out_specs=(VM, VM),
        compiler_params=params(),
        name="assemble",
    )(*blocks)


def hop_kernel(dz_ref, _, came, out, sem):
    copies = []
    for z in range(NZ):
        cp = pltpu.make_async_copy(
            came.at[(z - dz_ref[0]) & (NZ - 1), pl.ds(SLOT1 - HOP, HOP)],
            out.at[z, pl.ds(SLOT2 - HOP, HOP)],
            sem.at[z],
        )
        cp.start()
        copies.append(cp)
    for cp in copies:
        cp.wait()


def hop(dz, zs, came):
    return pl.pallas_call(
        hop_kernel,
        out_shape=jax.ShapeDtypeStruct(zs.shape, zs.dtype),
        in_specs=[SM, HB, HB],
        out_specs=HB,
        scratch_shapes=[pltpu.SemaphoreType.DMA((NZ,))],
        input_output_aliases={1: 0},
        compiler_params=params(),
        name="hop",
    )(dz, zs, came)


def unpack_kv_kernel(idx_ref, b0, b1, b2, b3, out_ref, held):
    for k, b in enumerate((b0, b1, b2, b3)):
        held[k * NZ * PER:(k + 1) * NZ * PER] = b[...]

    def step(p, carry):
        out_ref[p] = held[idx_ref[p]]
        return carry

    lax.fori_loop(0, ROWS, step, 0, unroll=8)


def unpack_kv(idx, blocks):
    return pl.pallas_call(
        unpack_kv_kernel,
        out_shape=jax.ShapeDtypeStruct((ROWS, KV, UNIT, HD), BF),
        in_specs=[SM] + [VM] * NY,
        out_specs=VM,
        scratch_shapes=[pltpu.VMEM((ROWS, KV, UNIT, HD), BF)],
        compiler_params=params(),
        name="unpack_kv",
    )(idx, *blocks)


def window_kernel(at_ref, n2, n1, n0, m2, m1, m0, h2, h1a, h1b, h0, e2, e1, e0, out_ref, seg_ref):
    out_ref[:ROWS] = h2[...]
    out_ref[ROWS:2 * ROWS] = h1a[...] + h1b[...]
    out_ref[2 * ROWS:] = h0[...]
    for k, (n, e) in enumerate(((n2, e2), (n1, e1), (n0, e0))):
        for i in range(3):
            out_ref[k * ROWS + n[ROWS + i]] = e[i]
    at = at_ref[0]
    seg_ref[:, :ROWS] = jnp.where(at >= 2, m2[:, :ROWS], -1)
    seg_ref[:, ROWS:2 * ROWS] = jnp.where(at >= 1, m1[:, :ROWS], -1)
    seg_ref[:, 2 * ROWS:] = m0[:, :ROWS]


def window(at, notes, rows, extra):
    wide = lambda a: a.reshape(-1, KV * UNIT, HD)
    return pl.pallas_call(
        window_kernel,
        out_shape=(
            jax.ShapeDtypeStruct((3 * ROWS, KV * UNIT, HD), BF),
            jax.ShapeDtypeStruct((1, 3 * ROWS), jnp.int32),
        ),
        in_specs=[SM] * 4 + [VM] * 10,
        out_specs=(VM, VM),
        compiler_params=params(),
        name="window",
    )(at, *notes, *[n[None] for n in notes], *map(wide, rows), *map(wide, extra))


def unpack_q_kernel(first, units, idx_ref, note_ref, src_ref, ext_ref, *rest):
    out_ref = rest[-1]

    def step(p, carry):
        out_ref[p] = src_ref[pl.ds(idx_ref[p], units)]
        return carry

    lax.fori_loop(0, ROWS, step, 0, unroll=16)
    for e in range(3):
        out_ref[note_ref[ROWS + e]] = ext_ref[e, first:first + units]


def unpack_q(first, units, idx, note, zr, ext, *after):
    rows = pl.pallas_call(
        functools.partial(unpack_q_kernel, first, units),
        out_shape=jax.ShapeDtypeStruct((ROWS, units, UNIT, HD), BF),
        in_specs=[SM, SM, VM, VM] + [VM] * len(after),
        out_specs=VM,
        compiler_params=params(),
        name="unpack_q",
    )(idx, note, zr.reshape(-1, UNIT, HD), ext, *after)
    return rows.reshape(ROWS, units * UNIT, HD).transpose(1, 0, 2)


def attend_kernel(part, heads, scale, q_ref, kv_ref, segq_ref, segk_ref, *rest):
    if part == 0:
        out_hbm, done_ref, held, sem = rest
        done_ref[...] = jnp.zeros_like(done_ref)
    else:
        _, out_hbm, held, sem = rest
    base = part * QA
    blocks = []
    for lo, rows in ((0, 128), (128, 64)):
        span = min(rows + 2 * ROWS, 3 * ROWS - lo)
        i = lax.broadcasted_iota(jnp.int32, (rows, span), 0)
        j = lax.broadcasted_iota(jnp.int32, (rows, span), 1)
        seen = (segq_ref[lo:lo + rows, :] == segk_ref[:, lo:lo + span]) & (j <= i + 2 * ROWS)
        blocks.append((lo, rows, span, seen))
    units = [(h, b) for h in range(heads) for b in range(len(blocks))]

    def scores(h, b):
        lo, rows, span, _ = blocks[b]
        q = q_ref[4 * h:4 * h + 4, lo:lo + rows].reshape(4 * rows, HD)
        keys = kv_ref[2 * (base + h), lo:lo + span]
        return lax.dot_general(q, keys, (((1,), (1,)), ((), ())), preferred_element_type=jnp.float32)

    copies = []
    later = scores(*units[0])
    for n, (h, b) in enumerate(units):
        lo, rows, span, seen = blocks[b]
        s = later
        if n + 1 < len(units):
            later = scores(*units[n + 1])
        s = jnp.where(seen[None], s.reshape(4, rows, span), -jnp.inf).reshape(4 * rows, span)
        w = jnp.exp2((s - jnp.max(s, axis=1, keepdims=True)) * (scale * math.log2(math.e)))
        total = jnp.sum(w, axis=1, keepdims=True)
        values = kv_ref[2 * (base + h) + 1, lo:lo + span]
        o = jnp.dot(w.astype(BF), values, preferred_element_type=jnp.float32)
        o = (o / total).astype(BF)
        for g in range(4):
            held[h, lo:lo + rows, g * HD:(g + 1) * HD] = o[g * rows:(g + 1) * rows]
        if b == len(blocks) - 1:
            first = (base + h) * 4 * HD
            cp = pltpu.make_async_copy(held.at[h], out_hbm.at[:, first:first + 4 * HD], sem.at[h])
            cp.start()
            copies.append(cp)
    for cp in copies:
        cp.wait()


def attend(part, qt, kvt, segq, segk, *prior):
    heads = QB if part else QA
    whole = jax.ShapeDtypeStruct((ROWS, (QA + QB) * UNIT * HD), BF)
    return pl.pallas_call(
        functools.partial(attend_kernel, part, heads, HD ** -0.5),
        out_shape=(whole, jax.ShapeDtypeStruct((8, HD), jnp.float32)) if part == 0 else whole,
        in_specs=[VM] * 4 + [HB] * len(prior),
        out_specs=(HB, VM) if part == 0 else HB,
        scratch_shapes=[pltpu.VMEM((heads, ROWS, 4 * HD), BF), pltpu.SemaphoreType.DMA((heads,))],
        input_output_aliases={4: 0} if prior else {},
        compiler_params=params(32),
        cost_estimate=pl.CostEstimate(
            flops=16 * ROWS * 576 * heads * HD, bytes_accessed=4 << 20, transcendentals=4 * ROWS * 576 * heads
        ),
        name="attend",
    )(qt, kvt, segq, segk, *prior)


def on_device(queries, key_value, route_group, arrive_slot, segment_ids):
    z, y, s = lax.axis_index("z"), lax.axis_index("y"), lax.axis_index("seq")
    kv = key_value.reshape(ROWS, KV, UNIT, HD)
    up = lambda a, n: lax.ppermute(a, "seq", [(i, i + n) for i in range(NS - n)])
    side = lambda a, n: lax.ppermute(a, "y", [(i, (i + n) % NY) for i in range(NY)])

    src, rank = arrive_slot // 6, arrive_slot % 6
    sy, sz = src & (NY - 1), src >> 2
    over = rank >= PER
    dy = (y - sy) & (NY - 1)
    idx1 = jnp.where(over, 0, (dy * NZ + sz) * PER + rank)
    idx2 = jnp.where(over, 0, sz * SLOT2 + (dy * PER + rank) * QA)
    idx3 = jnp.where(over, 0, sz * SLOT3 + (dy * PER + rank) * QB)

    place = jnp.arange(ROWS, dtype=jnp.int32)
    pos = jnp.stack([jnp.sum(jnp.where(rank == PER + e, place, 0)) for e in range(3)])
    note = jnp.concatenate([segment_ids.reshape(ROWS), pos])
    note1, note2 = up(note, 1), up(note, 2)

    zs1, tile, meta = pack_kv(y.reshape(1), route_group, kv, queries)
    k6 = (meta[0] - (z * NY + y)) & (NZ * NY - 1)
    dz = (((y + k6) >> 2) & (NZ - 1)).reshape(1)
    zr1 = lax.all_to_all(zs1.reshape(NZ, SLOT1, UNIT, HD), "z", 0, 0, tiled=True)

    tile, queries = lax.optimization_barrier((tile, queries))
    qy = pack_q(tile, queries.reshape(ROWS, QA + QB, UNIT, HD))
    n = NZ * PER
    qy = [qy[:n]] + [side(qy[k * n:(k + 1) * n], k) for k in range(1, NY)]
    zs2, zs3 = assemble(qy)
    zs2, zs3, note1, note2, dz = lax.optimization_barrier((zs2, zs3, note1, note2, dz))
    zr2 = lax.all_to_all(hop(dz, zs2, zr1), "z", 0, 0, tiled=True)

    run = PER * KV
    part = [zr1[:, k * run:(k + 1) * run].reshape(NZ * PER, KV, UNIT, HD) for k in range(NY)]
    own = unpack_kv(idx1, [part[0]] + [side(part[k], k) for k in range(1, NY)])
    own2 = up(own, 2)
    own1a = lax.ppermute(own, "seq", [(i, i + 1) for i in range(0, NS, 2)])
    zs3, own2, own1a = lax.optimization_barrier((zs3, own2, own1a))
    own1b = lax.ppermute(own2, "seq", [(i + 1, i) for i in range(0, NS, 2)])
    zr3 = lax.all_to_all(zs3, "z", 0, 0, tiled=True)

    came = zr2[:EXT // HOP, SLOT2 - HOP:].reshape(EXT, UNIT, HD)
    came = jnp.where((k6 & 1) != 0, side(came, 1), came)
    came = jnp.where((k6 & 2) != 0, side(came, 2), came)
    ext = came.reshape(3, EXT // 3, UNIT, HD)
    ext0 = ext[:, :KV]
    rows, segk = window(
        s.reshape(1), (note2, note1, note), (own2, own1a, own1b, own), (up(ext0, 2), up(ext0, 1), ext0)
    )
    kvt, segq = rows.transpose(1, 0, 2), segment_ids.reshape(ROWS, 1)
    out, done = attend(0, unpack_q(KV, QA, idx2, note, zr2, ext), kvt, segq, segk)
    return attend(1, unpack_q(KV + QA, QB, idx3, note, zr3, ext, done), kvt, segq, segk, out)


def solution(mesh):
    fine = Mesh(mesh.devices.reshape(NZ, NY, NS), ("z", "y", "seq"))
    rows = ("z", "y", "seq")
    return jax.shard_map(
        on_device,
        mesh=fine,
        in_specs=(
            P(rows, None),
            P(rows, None, None, None),
            P(rows),
            P(rows),
            P(("z", "y"), "seq"),
        ),
        out_specs=P(rows, None),
        check_vma=False,
    )
```

```python
import functools
import math

import jax
import jax.numpy as jnp
from jax import lax
from jax.experimental import pallas as pl
from jax.experimental.pallas import tpu as pltpu
from jax.sharding import Mesh, PartitionSpec as P

ROWS = 192
NZ, NY, NS = 16, 4, 8
PER = 3
HD = 128
UNIT = 4
KV, QA, QB = 4, 5, 3
BASE = NY * PER
HOP = 3
EXT = 3 * (KV + QA + QB)
SLOT1, SLOT2, SLOT3 = BASE * KV + HOP, BASE * QA + HOP, BASE * QB
BF = jnp.bfloat16
MIB = 1024 * 1024

VM = pl.BlockSpec(memory_space=pltpu.VMEM)
SM = pl.BlockSpec(memory_space=pltpu.SMEM)
HB = pl.BlockSpec(memory_space=pltpu.HBM)


def params(mib=16):
    return pltpu.CompilerParams(vmem_limit_bytes=mib * MIB)


def pack_kv_kernel(me_ref, rg_hbm, kv_hbm, q_hbm, out_hbm, tile_ref, meta_ref, rg, nxt, xrow, kvs, qs, held, sem):
    plan = pltpu.make_async_copy(rg_hbm, rg, sem.at[0])
    plan.start()
    load = pltpu.make_async_copy(kv_hbm, kvs, sem.at[1])
    load.start()
    load_q = pltpu.make_async_copy(q_hbm, qs, sem.at[2])
    load_q.start()
    y = me_ref[0]
    for d in range(NZ * NY):
        nxt[d] = (d // NY * 64 + ((d % NY - y) & (NY - 1)) * PER * KV) * 8
    for e in range(4):
        xrow[e] = 0
    plan.wait()

    def step(i, far):
        d = rg[i]
        n = nxt[d]
        r = n & 7
        nxt[d] = n + KV * 8 + 1
        over = r >= PER
        tile_ref[i] = jnp.where(over, NZ * 64, n >> 3)
        xrow[jnp.where(over, r - PER, 3)] = i
        return jnp.where(over, d, far)

    meta_ref[0] = lax.fori_loop(0, ROWS, step, 0, unroll=16)
    load.wait()

    def move(i, carry):
        t = tile_ref[i]
        held[t >> 6, pl.ds(t & 63, KV)] = kvs[i]
        return carry

    lax.fori_loop(0, ROWS, move, 0, unroll=16)
    base = pltpu.make_async_copy(
        held.at[pl.ds(0, NZ), pl.ds(0, BASE * KV)], out_hbm.at[:, pl.ds(0, BASE * KV)], sem.at[3]
    )
    base.start()
    load_q.wait()
    row = lax.broadcasted_iota(jnp.int32, (16, (QA + QB) * UNIT * HD), 0)

    def place(e, u):
        j = e * (KV + QA + QB) + u
        return j // HOP, BASE * KV + j % HOP

    for e in range(3):
        for u in range(KV):
            held[place(e, u)] = kvs[xrow[e], u]
        first = pl.multiple_of((xrow[e] >> 4) << 4, 16)
        block = qs[pl.ds(first, 16), :].astype(jnp.float32)
        one = jnp.sum(jnp.where(row == (xrow[e] & 15), block, 0.0), axis=0, keepdims=True)
        for u in range(QA + QB):
            parts = [one[:, (u * UNIT + c) * HD:(u * UNIT + c + 1) * HD] for c in range(UNIT)]
            held[place(e, KV + u)] = jnp.concatenate(parts, axis=0).astype(BF)
    more = pltpu.make_async_copy(
        held.at[pl.ds(0, NZ), pl.ds(BASE * KV, HOP)], out_hbm.at[:, pl.ds(BASE * KV, HOP)], sem.at[4]
    )
    more.start()
    base.wait()
    more.wait()


def pack_kv(me, rg, kv, q):
    return pl.pallas_call(
        pack_kv_kernel,
        out_shape=(
            jax.ShapeDtypeStruct((NZ, SLOT1, UNIT, HD), BF),
            jax.ShapeDtypeStruct((ROWS,), jnp.int32),
            jax.ShapeDtypeStruct((1,), jnp.int32),
        ),
        in_specs=[SM, HB, HB, HB],
        out_specs=(HB, SM, SM),
        scratch_shapes=[
            pltpu.SMEM((ROWS,), jnp.int32),
            pltpu.SMEM((NZ * NY,), jnp.int32),
            pltpu.SMEM((4,), jnp.int32),
            pltpu.VMEM((ROWS, KV, UNIT, HD), BF),
            pltpu.VMEM((ROWS, (QA + QB) * UNIT * HD), BF),
            pltpu.VMEM((NZ + 1, SLOT1, UNIT, HD), BF),
            pltpu.SemaphoreType.DMA((5,)),
        ],
        compiler_params=params(60),
        name="pack_kv",
    )(me, rg, kv, q)


def pack_q_kernel(tile_ref, q_ref, out_ref):
    out_ref[...] = jnp.zeros_like(out_ref)

    def step(i, carry):
        t = tile_ref[i]
        gz = t >> 6
        k = (t & 63) >> 2
        dy = (k * 11) >> 5
        out_ref[jnp.where(gz == NZ, ROWS, (dy * NZ + gz) * PER + k - dy * PER)] = q_ref[i]
        return carry

    lax.fori_loop(0, ROWS, step, 0, unroll=16)


def pack_q(tile, q):
    return pl.pallas_call(
        pack_q_kernel,
        out_shape=jax.ShapeDtypeStruct((ROWS + 1, QA + QB, UNIT, HD), BF),
        in_specs=[SM, VM],
        out_specs=VM,
        compiler_params=params(),
        name="pack_q",
    )(tile, q)


def assemble_kernel(b0, b1, b2, b3, a_ref, b_ref):
    for k, b in enumerate((b0, b1, b2, b3)):

        def step(z, carry, k=k, b=b):
            for r in range(PER):
                a_ref[z, (k * PER + r) * QA:(k * PER + r + 1) * QA] = b[z * PER + r, :QA]
                b_ref[z, (k * PER + r) * QB:(k * PER + r + 1) * QB] = b[z * PER + r, QA:]
            return carry

        lax.fori_loop(0, NZ, step, 0, unroll=4)
    a_ref[:, SLOT2 - HOP:] = jnp.zeros((NZ, HOP, UNIT, HD), BF)


def assemble(blocks):
    return pl.pallas_call(
        assemble_kernel,
        out_shape=(
            jax.ShapeDtypeStruct((NZ, SLOT2, UNIT, HD), BF),
            jax.ShapeDtypeStruct((NZ, SLOT3, UNIT, HD), BF),
        ),
        in_specs=[VM] * NY,
        out_specs=(VM, VM),
        compiler_params=params(),
        name="assemble",
    )(*blocks)


def hop_kernel(dz_ref, _, came, out, sem):
    copies = []
    for z in range(NZ):
        cp = pltpu.make_async_copy(
            came.at[(z - dz_ref[0]) & (NZ - 1), pl.ds(SLOT1 - HOP, HOP)],
            out.at[z, pl.ds(SLOT2 - HOP, HOP)],
            sem.at[z],
        )
        cp.start()
        copies.append(cp)
    for cp in copies:
        cp.wait()


def hop(dz, zs, came):
    return pl.pallas_call(
        hop_kernel,
        out_shape=jax.ShapeDtypeStruct(zs.shape, zs.dtype),
        in_specs=[SM, HB, HB],
        out_specs=HB,
        scratch_shapes=[pltpu.SemaphoreType.DMA((NZ,))],
        input_output_aliases={1: 0},
        compiler_params=params(),
        name="hop",
    )(dz, zs, came)


def unpack_kv_kernel(idx_ref, b0, b1, b2, b3, out_ref, held):
    for k, b in enumerate((b0, b1, b2, b3)):
        held[k * NZ * PER:(k + 1) * NZ * PER] = b[...]

    def step(p, carry):
        out_ref[p] = held[idx_ref[p]]
        return carry

    lax.fori_loop(0, ROWS, step, 0, unroll=8)


def unpack_kv(idx, blocks):
    return pl.pallas_call(
        unpack_kv_kernel,
        out_shape=jax.ShapeDtypeStruct((ROWS, KV, UNIT, HD), BF),
        in_specs=[SM] + [VM] * NY,
        out_specs=VM,
        scratch_shapes=[pltpu.VMEM((ROWS, KV, UNIT, HD), BF)],
        compiler_params=params(),
        name="unpack_kv",
    )(idx, *blocks)


def window_kernel(at_ref, n2, n1, n0, m2, m1, m0, h2, h1a, h1b, h0, e2, e1, e0, out_ref, seg_ref):
    out_ref[:ROWS] = h2[...]
    out_ref[ROWS:2 * ROWS] = h1a[...] + h1b[...]
    out_ref[2 * ROWS:] = h0[...]
    for k, (n, e) in enumerate(((n2, e2), (n1, e1), (n0, e0))):
        for i in range(3):
            out_ref[k * ROWS + n[ROWS + i]] = e[i]
    at = at_ref[0]
    seg_ref[:, :ROWS] = jnp.where(at >= 2, m2[:, :ROWS], -1)
    seg_ref[:, ROWS:2 * ROWS] = jnp.where(at >= 1, m1[:, :ROWS], -1)
    seg_ref[:, 2 * ROWS:] = m0[:, :ROWS]


def window(at, notes, rows, extra):
    wide = lambda a: a.reshape(-1, KV * UNIT, HD)
    return pl.pallas_call(
        window_kernel,
        out_shape=(
            jax.ShapeDtypeStruct((3 * ROWS, KV * UNIT, HD), BF),
            jax.ShapeDtypeStruct((1, 3 * ROWS), jnp.int32),
        ),
        in_specs=[SM] * 4 + [VM] * 10,
        out_specs=(VM, VM),
        compiler_params=params(),
        name="window",
    )(at, *notes, *[n[None] for n in notes], *map(wide, rows), *map(wide, extra))


def unpack_q_kernel(first, units, idx_ref, note_ref, src_ref, ext_ref, *rest):
    out_ref = rest[-1]

    def step(p, carry):
        out_ref[p] = src_ref[pl.ds(idx_ref[p], units)]
        return carry

    lax.fori_loop(0, ROWS, step, 0, unroll=16)
    for e in range(3):
        out_ref[note_ref[ROWS + e]] = ext_ref[e, first:first + units]


def unpack_q(first, units, idx, note, zr, ext, *after):
    rows = pl.pallas_call(
        functools.partial(unpack_q_kernel, first, units),
        out_shape=jax.ShapeDtypeStruct((ROWS, units, UNIT, HD), BF),
        in_specs=[SM, SM, VM, VM] + [VM] * len(after),
        out_specs=VM,
        compiler_params=params(),
        name="unpack_q",
    )(idx, note, zr.reshape(-1, UNIT, HD), ext, *after)
    return rows.reshape(ROWS, units * UNIT, HD).transpose(1, 0, 2)


def attend_kernel(part, heads, scale, q_ref, kv_ref, segq_ref, segk_ref, *rest):
    if part == 0:
        out_hbm, done_ref, held, sem = rest
        done_ref[...] = jnp.zeros_like(done_ref)
    else:
        _, out_hbm, held, sem = rest
    base = part * QA
    blocks = []
    for lo, rows in ((0, 128), (128, 64)):
        span = min(rows + 2 * ROWS, 3 * ROWS - lo)
        i = lax.broadcasted_iota(jnp.int32, (rows, span), 0)
        j = lax.broadcasted_iota(jnp.int32, (rows, span), 1)
        seen = (segq_ref[lo:lo + rows, :] == segk_ref[:, lo:lo + span]) & (j <= i + 2 * ROWS)
        blocks.append((lo, rows, span, seen))
    units = [(h, b) for h in range(heads) for b in range(len(blocks))]

    def scores(h, b):
        lo, rows, span, _ = blocks[b]
        q = q_ref[4 * h:4 * h + 4, lo:lo + rows].reshape(4 * rows, HD)
        keys = kv_ref[2 * (base + h), lo:lo + span]
        return lax.dot_general(q, keys, (((1,), (1,)), ((), ())), preferred_element_type=jnp.float32)

    copies = []
    later = scores(*units[0])
    for n, (h, b) in enumerate(units):
        lo, rows, span, seen = blocks[b]
        s = later
        if n + 1 < len(units):
            later = scores(*units[n + 1])
        s = jnp.where(seen[None], s.reshape(4, rows, span), -jnp.inf).reshape(4 * rows, span)
        w = jnp.exp2((s - jnp.max(s, axis=1, keepdims=True)) * (scale * math.log2(math.e)))
        total = jnp.sum(w, axis=1, keepdims=True)
        values = kv_ref[2 * (base + h) + 1, lo:lo + span]
        o = jnp.dot(w.astype(BF), values, preferred_element_type=jnp.float32)
        o = (o / total).astype(BF)
        for g in range(4):
            held[h, lo:lo + rows, g * HD:(g + 1) * HD] = o[g * rows:(g + 1) * rows]
        if b == len(blocks) - 1:
            first = (base + h) * 4 * HD
            cp = pltpu.make_async_copy(held.at[h], out_hbm.at[:, first:first + 4 * HD], sem.at[h])
            cp.start()
            copies.append(cp)
    for cp in copies:
        cp.wait()


def attend(part, qt, kvt, segq, segk, *prior):
    heads = QB if part else QA
    whole = jax.ShapeDtypeStruct((ROWS, (QA + QB) * UNIT * HD), BF)
    return pl.pallas_call(
        functools.partial(attend_kernel, part, heads, HD ** -0.5),
        out_shape=(whole, jax.ShapeDtypeStruct((8, HD), jnp.float32)) if part == 0 else whole,
        in_specs=[VM] * 4 + [HB] * len(prior),
        out_specs=(HB, VM) if part == 0 else HB,
        scratch_shapes=[pltpu.VMEM((heads, ROWS, 4 * HD), BF), pltpu.SemaphoreType.DMA((heads,))],
        input_output_aliases={4: 0} if prior else {},
        compiler_params=params(32),
        cost_estimate=pl.CostEstimate(
            flops=16 * ROWS * 576 * heads * HD, bytes_accessed=4 << 20, transcendentals=4 * ROWS * 576 * heads
        ),
        name="attend",
    )(qt, kvt, segq, segk, *prior)


def on_device(queries, key_value, route_group, arrive_slot, segment_ids):
    z, y, s = lax.axis_index("z"), lax.axis_index("y"), lax.axis_index("seq")
    kv = key_value.reshape(ROWS, KV, UNIT, HD)
    up = lambda a, n: lax.ppermute(a, "seq", [(i, i + n) for i in range(NS - n)])
    side = lambda a, n: lax.ppermute(a, "y", [(i, (i + n) % NY) for i in range(NY)])

    src, rank = arrive_slot // 6, arrive_slot % 6
    sy, sz = src & (NY - 1), src >> 2
    over = rank >= PER
    dy = (y - sy) & (NY - 1)
    idx1 = jnp.where(over, 0, (dy * NZ + sz) * PER + rank)
    idx2 = jnp.where(over, 0, sz * SLOT2 + (dy * PER + rank) * QA)
    idx3 = jnp.where(over, 0, sz * SLOT3 + (dy * PER + rank) * QB)

    place = jnp.arange(ROWS, dtype=jnp.int32)
    pos = jnp.stack([jnp.sum(jnp.where(rank == PER + e, place, 0)) for e in range(3)])
    note = jnp.concatenate([segment_ids.reshape(ROWS), pos])
    note1, note2 = up(note, 1), up(note, 2)

    zs1, tile, meta = pack_kv(y.reshape(1), route_group, kv, queries)
    k6 = (meta[0] - (z * NY + y)) & (NZ * NY - 1)
    dz = (((y + k6) >> 2) & (NZ - 1)).reshape(1)
    zr1 = lax.all_to_all(zs1, "z", 0, 0, tiled=True)

    tile, queries = lax.optimization_barrier((tile, queries))
    qy = pack_q(tile, queries.reshape(ROWS, QA + QB, UNIT, HD))
    n = NZ * PER
    qy = [qy[:n]] + [side(qy[k * n:(k + 1) * n], k) for k in range(1, NY)]
    zs2, zs3 = assemble(qy)
    zs2, zs3, note1, note2, dz = lax.optimization_barrier((zs2, zs3, note1, note2, dz))
    zr2 = lax.all_to_all(hop(dz, zs2, zr1), "z", 0, 0, tiled=True)

    run = PER * KV
    part = [zr1[:, k * run:(k + 1) * run].reshape(NZ * PER, KV, UNIT, HD) for k in range(NY)]
    own = unpack_kv(idx1, [part[0]] + [side(part[k], k) for k in range(1, NY)])
    own2 = up(own, 2)
    own1a = lax.ppermute(own, "seq", [(i, i + 1) for i in range(0, NS, 2)])
    own1b = lax.ppermute(own2, "seq", [(i + 1, i) for i in range(0, NS, 2)])
    zs3, own2, own1a, own1b = lax.optimization_barrier((zs3, own2, own1a, own1b))
    zr3 = lax.all_to_all(zs3, "z", 0, 0, tiled=True)

    came = zr2[:EXT // HOP, SLOT2 - HOP:].reshape(EXT, UNIT, HD)
    came = jnp.where((k6 & 1) != 0, side(came, 1), came)
    came = jnp.where((k6 & 2) != 0, side(came, 2), came)
    ext = came.reshape(3, EXT // 3, UNIT, HD)
    ext0 = ext[:, :KV]
    rows, segk = window(
        s.reshape(1), (note2, note1, note), (own2, own1a, own1b, own), (up(ext0, 2), up(ext0, 1), ext0)
    )
    kvt, segq = rows.transpose(1, 0, 2), segment_ids.reshape(ROWS, 1)
    out, done = attend(0, unpack_q(KV, QA, idx2, note, zr2, ext), kvt, segq, segk)
    return attend(1, unpack_q(KV + QA, QB, idx3, note, zr3, ext, done), kvt, segq, segk, out)


def solution(mesh):
    fine = Mesh(mesh.devices.reshape(NZ, NY, NS), ("z", "y", "seq"))
    rows = ("z", "y", "seq")
    return jax.shard_map(
        on_device,
        mesh=fine,
        in_specs=(
            P(rows, None),
            P(rows, None, None, None),
            P(rows),
            P(rows),
            P(("z", "y"), "seq"),
        ),
        out_specs=P(rows, None),
        check_vma=False,
    )
```

```python
import functools
import math

import jax
import jax.numpy as jnp
from jax import lax
from jax.experimental import pallas as pl
from jax.experimental.pallas import tpu as pltpu
from jax.sharding import Mesh, PartitionSpec as P

ROWS = 192
NZ, NY, NS = 16, 4, 8
PER = 3
HD = 128
UNIT = 4
KV, QA, QB = 4, 5, 3
BASE = NY * PER
HOP = 3
EXT = 3 * (KV + QA + QB)
SLOT1, SLOT2, SLOT3 = BASE * KV + HOP, BASE * QA + HOP, BASE * QB
BF = jnp.bfloat16
MIB = 1024 * 1024

VM = pl.BlockSpec(memory_space=pltpu.VMEM)
SM = pl.BlockSpec(memory_space=pltpu.SMEM)
HB = pl.BlockSpec(memory_space=pltpu.HBM)


def params(mib=16):
    return pltpu.CompilerParams(vmem_limit_bytes=mib * MIB)


def pack_kv_kernel(me_ref, rg_hbm, kv_hbm, q_hbm, out_hbm, tile_ref, meta_ref, rg, nxt, xrow, kvs, qs, held, sem):
    plan = pltpu.make_async_copy(rg_hbm, rg, sem.at[0])
    plan.start()
    load = pltpu.make_async_copy(kv_hbm, kvs, sem.at[1])
    load.start()
    load_q = pltpu.make_async_copy(q_hbm, qs, sem.at[2])
    load_q.start()
    y = me_ref[0]
    for d in range(NZ * NY):
        nxt[d] = (d // NY * 64 + ((d % NY - y) & (NY - 1)) * PER * KV) * 8
    for e in range(4):
        xrow[e] = 0
    plan.wait()

    def step(i, far):
        d = rg[i]
        n = nxt[d]
        r = n & 7
        nxt[d] = n + KV * 8 + 1
        over = r >= PER
        t = jnp.where(over, NZ * 64, n >> 3)
        tile_ref[i] = t
        held[t >> 6, pl.ds(t & 63, KV)] = kvs[i]
        xrow[jnp.where(over, r - PER, 3)] = i
        return jnp.where(over, d, far)

    load.wait()
    meta_ref[0] = lax.fori_loop(0, ROWS, step, 0, unroll=16)
    base = pltpu.make_async_copy(
        held.at[pl.ds(0, NZ), pl.ds(0, BASE * KV)], out_hbm.at[:, pl.ds(0, BASE * KV)], sem.at[3]
    )
    base.start()
    load_q.wait()
    row = lax.broadcasted_iota(jnp.int32, (16, (QA + QB) * UNIT * HD), 0)

    def place(e, u):
        j = e * (KV + QA + QB) + u
        return j // HOP, BASE * KV + j % HOP

    for e in range(3):
        for u in range(KV):
            held[place(e, u)] = kvs[xrow[e], u]
        first = pl.multiple_of((xrow[e] >> 4) << 4, 16)
        block = qs[pl.ds(first, 16), :].astype(jnp.float32)
        one = jnp.sum(jnp.where(row == (xrow[e] & 15), block, 0.0), axis=0, keepdims=True)
        for u in range(QA + QB):
            parts = [one[:, (u * UNIT + c) * HD:(u * UNIT + c + 1) * HD] for c in range(UNIT)]
            held[place(e, KV + u)] = jnp.concatenate(parts, axis=0).astype(BF)
    more = pltpu.make_async_copy(
        held.at[pl.ds(0, NZ), pl.ds(BASE * KV, HOP)], out_hbm.at[:, pl.ds(BASE * KV, HOP)], sem.at[4]
    )
    more.start()
    base.wait()
    more.wait()


def pack_kv(me, rg, kv, q):
    return pl.pallas_call(
        pack_kv_kernel,
        out_shape=(
            jax.ShapeDtypeStruct((NZ, SLOT1, UNIT, HD), BF),
            jax.ShapeDtypeStruct((ROWS,), jnp.int32),
            jax.ShapeDtypeStruct((1,), jnp.int32),
        ),
        in_specs=[SM, HB, HB, HB],
        out_specs=(HB, SM, SM),
        scratch_shapes=[
            pltpu.SMEM((ROWS,), jnp.int32),
            pltpu.SMEM((NZ * NY,), jnp.int32),
            pltpu.SMEM((4,), jnp.int32),
            pltpu.VMEM((ROWS, KV, UNIT, HD), BF),
            pltpu.VMEM((ROWS, (QA + QB) * UNIT * HD), BF),
            pltpu.VMEM((NZ + 1, SLOT1, UNIT, HD), BF),
            pltpu.SemaphoreType.DMA((5,)),
        ],
        compiler_params=params(60),
        name="pack_kv",
    )(me, rg, kv, q)


def pack_q_kernel(tile_ref, q_ref, out_ref):
    out_ref[...] = jnp.zeros_like(out_ref)

    def step(i, carry):
        t = tile_ref[i]
        gz = t >> 6
        k = (t & 63) >> 2
        dy = (k * 11) >> 5
        out_ref[jnp.where(gz == NZ, ROWS, (dy * NZ + gz) * PER + k - dy * PER)] = q_ref[i]
        return carry

    lax.fori_loop(0, ROWS, step, 0, unroll=16)


def pack_q(tile, q):
    return pl.pallas_call(
        pack_q_kernel,
        out_shape=jax.ShapeDtypeStruct((ROWS + 1, QA + QB, UNIT, HD), BF),
        in_specs=[SM, VM],
        out_specs=VM,
        compiler_params=params(),
        name="pack_q",
    )(tile, q)


def assemble_kernel(b0, b1, b2, b3, a_ref, b_ref):
    for k, b in enumerate((b0, b1, b2, b3)):

        def step(z, carry, k=k, b=b):
            for r in range(PER):
                a_ref[z, (k * PER + r) * QA:(k * PER + r + 1) * QA] = b[z * PER + r, :QA]
                b_ref[z, (k * PER + r) * QB:(k * PER + r + 1) * QB] = b[z * PER + r, QA:]
            return carry

        lax.fori_loop(0, NZ, step, 0, unroll=4)
    a_ref[:, SLOT2 - HOP:] = jnp.zeros((NZ, HOP, UNIT, HD), BF)


def assemble(blocks):
    return pl.pallas_call(
        assemble_kernel,
        out_shape=(
            jax.ShapeDtypeStruct((NZ, SLOT2, UNIT, HD), BF),
            jax.ShapeDtypeStruct((NZ, SLOT3, UNIT, HD), BF),
        ),
        in_specs=[VM] * NY,
        out_specs=(VM, VM),
        compiler_params=params(),
        name="assemble",
    )(*blocks)


def hop_kernel(dz_ref, _, came, out, sem):
    copies = []
    for z in range(NZ):
        cp = pltpu.make_async_copy(
            came.at[(z - dz_ref[0]) & (NZ - 1), pl.ds(SLOT1 - HOP, HOP)],
            out.at[z, pl.ds(SLOT2 - HOP, HOP)],
            sem.at[z],
        )
        cp.start()
        copies.append(cp)
    for cp in copies:
        cp.wait()


def hop(dz, zs, came):
    return pl.pallas_call(
        hop_kernel,
        out_shape=jax.ShapeDtypeStruct(zs.shape, zs.dtype),
        in_specs=[SM, HB, HB],
        out_specs=HB,
        scratch_shapes=[pltpu.SemaphoreType.DMA((NZ,))],
        input_output_aliases={1: 0},
        compiler_params=params(),
        name="hop",
    )(dz, zs, came)


def unpack_kv_kernel(idx_ref, b0, b1, b2, b3, out_ref, held):
    for k, b in enumerate((b0, b1, b2, b3)):
        held[k * NZ * PER:(k + 1) * NZ * PER] = b[...]

    def step(p, carry):
        out_ref[p] = held[idx_ref[p]]
        return carry

    lax.fori_loop(0, ROWS, step, 0, unroll=8)


def unpack_kv(idx, blocks):
    return pl.pallas_call(
        unpack_kv_kernel,
        out_shape=jax.ShapeDtypeStruct((ROWS, KV, UNIT, HD), BF),
        in_specs=[SM] + [VM] * NY,
        out_specs=VM,
        scratch_shapes=[pltpu.VMEM((ROWS, KV, UNIT, HD), BF)],
        compiler_params=params(),
        name="unpack_kv",
    )(idx, *blocks)


def window_kernel(at_ref, n2, n1, n0, m2, m1, m0, h2, h1a, h1b, h0, e2, e1, e0, out_ref, seg_ref):
    out_ref[:ROWS] = h2[...]
    out_ref[ROWS:2 * ROWS] = h1a[...] + h1b[...]
    out_ref[2 * ROWS:] = h0[...]
    for k, (n, e) in enumerate(((n2, e2), (n1, e1), (n0, e0))):
        for i in range(3):
            out_ref[k * ROWS + n[ROWS + i]] = e[i]
    at = at_ref[0]
    seg_ref[:, :ROWS] = jnp.where(at >= 2, m2[:, :ROWS], -1)
    seg_ref[:, ROWS:2 * ROWS] = jnp.where(at >= 1, m1[:, :ROWS], -1)
    seg_ref[:, 2 * ROWS:] = m0[:, :ROWS]


def window(at, notes, rows, extra):
    wide = lambda a: a.reshape(-1, KV * UNIT, HD)
    return pl.pallas_call(
        window_kernel,
        out_shape=(
            jax.ShapeDtypeStruct((3 * ROWS, KV * UNIT, HD), BF),
            jax.ShapeDtypeStruct((1, 3 * ROWS), jnp.int32),
        ),
        in_specs=[SM] * 4 + [VM] * 10,
        out_specs=(VM, VM),
        compiler_params=params(),
        name="window",
    )(at, *notes, *[n[None] for n in notes], *map(wide, rows), *map(wide, extra))


def unpack_q_kernel(first, units, idx_ref, note_ref, src_ref, ext_ref, *rest):
    out_ref = rest[-1]

    def step(p, carry):
        out_ref[p] = src_ref[pl.ds(idx_ref[p], units)]
        return carry

    lax.fori_loop(0, ROWS, step, 0, unroll=16)
    for e in range(3):
        out_ref[note_ref[ROWS + e]] = ext_ref[e, first:first + units]


def unpack_q(first, units, idx, note, zr, ext, *after):
    rows = pl.pallas_call(
        functools.partial(unpack_q_kernel, first, units),
        out_shape=jax.ShapeDtypeStruct((ROWS, units, UNIT, HD), BF),
        in_specs=[SM, SM, VM, VM] + [VM] * len(after),
        out_specs=VM,
        compiler_params=params(),
        name="unpack_q",
    )(idx, note, zr.reshape(-1, UNIT, HD), ext, *after)
    return rows.reshape(ROWS, units * UNIT, HD).transpose(1, 0, 2)


def attend_kernel(part, heads, scale, q_ref, kv_ref, segq_ref, segk_ref, *rest):
    if part == 0:
        out_hbm, done_ref, held, sem = rest
        done_ref[...] = jnp.zeros_like(done_ref)
    else:
        _, out_hbm, held, sem = rest
    base = part * QA
    blocks = []
    for lo, rows in ((0, 128), (128, 64)):
        span = min(rows + 2 * ROWS, 3 * ROWS - lo)
        i = lax.broadcasted_iota(jnp.int32, (rows, span), 0)
        j = lax.broadcasted_iota(jnp.int32, (rows, span), 1)
        seen = (segq_ref[lo:lo + rows, :] == segk_ref[:, lo:lo + span]) & (j <= i + 2 * ROWS)
        blocks.append((lo, rows, span, seen))
    units = [(h, b) for h in range(heads) for b in range(len(blocks))]

    def scores(h, b):
        lo, rows, span, _ = blocks[b]
        q = q_ref[4 * h:4 * h + 4, lo:lo + rows].reshape(4 * rows, HD)
        keys = kv_ref[2 * (base + h), lo:lo + span]
        return lax.dot_general(q, keys, (((1,), (1,)), ((), ())), preferred_element_type=jnp.float32)

    copies = []
    later = scores(*units[0])
    for n, (h, b) in enumerate(units):
        lo, rows, span, seen = blocks[b]
        s = later
        if n + 1 < len(units):
            later = scores(*units[n + 1])
        s = jnp.where(seen[None], s.reshape(4, rows, span), -jnp.inf).reshape(4 * rows, span)
        w = jnp.exp2((s - jnp.max(s, axis=1, keepdims=True)) * (scale * math.log2(math.e)))
        total = jnp.sum(w, axis=1, keepdims=True)
        values = kv_ref[2 * (base + h) + 1, lo:lo + span]
        o = jnp.dot(w.astype(BF), values, preferred_element_type=jnp.float32)
        o = (o / total).astype(BF)
        for g in range(4):
            held[h, lo:lo + rows, g * HD:(g + 1) * HD] = o[g * rows:(g + 1) * rows]
        first = (base + h) * 4 * HD
        cp = pltpu.make_async_copy(
            held.at[h, lo:lo + rows], out_hbm.at[lo:lo + rows, first:first + 4 * HD], sem.at[n]
        )
        cp.start()
        copies.append(cp)
    for cp in copies:
        cp.wait()


def attend(part, qt, kvt, segq, segk, *prior):
    heads = QB if part else QA
    whole = jax.ShapeDtypeStruct((ROWS, (QA + QB) * UNIT * HD), BF)
    return pl.pallas_call(
        functools.partial(attend_kernel, part, heads, HD ** -0.5),
        out_shape=(whole, jax.ShapeDtypeStruct((8, HD), jnp.float32)) if part == 0 else whole,
        in_specs=[VM] * 4 + [HB] * len(prior),
        out_specs=(HB, VM) if part == 0 else HB,
        scratch_shapes=[pltpu.VMEM((heads, ROWS, 4 * HD), BF), pltpu.SemaphoreType.DMA((2 * heads,))],
        input_output_aliases={4: 0} if prior else {},
        compiler_params=params(32),
        cost_estimate=pl.CostEstimate(
            flops=16 * ROWS * 576 * heads * HD, bytes_accessed=4 << 20, transcendentals=4 * ROWS * 576 * heads
        ),
        name="attend",
    )(qt, kvt, segq, segk, *prior)


def on_device(queries, key_value, route_group, arrive_slot, segment_ids):
    z, y, s = lax.axis_index("z"), lax.axis_index("y"), lax.axis_index("seq")
    kv = key_value.reshape(ROWS, KV, UNIT, HD)
    up = lambda a, n: lax.ppermute(a, "seq", [(i, i + n) for i in range(NS - n)])
    side = lambda a, n: lax.ppermute(a, "y", [(i, (i + n) % NY) for i in range(NY)])

    src, rank = arrive_slot // 6, arrive_slot % 6
    sy, sz = src & (NY - 1), src >> 2
    over = rank >= PER
    dy = (y - sy) & (NY - 1)
    idx1 = jnp.where(over, 0, (dy * NZ + sz) * PER + rank)
    idx2 = jnp.where(over, 0, sz * SLOT2 + (dy * PER + rank) * QA)
    idx3 = jnp.where(over, 0, sz * SLOT3 + (dy * PER + rank) * QB)

    place = jnp.arange(ROWS, dtype=jnp.int32)
    pos = jnp.stack([jnp.sum(jnp.where(rank == PER + e, place, 0)) for e in range(3)])
    note = jnp.concatenate([segment_ids.reshape(ROWS), pos])
    note1, note2 = up(note, 1), up(note, 2)

    zs1, tile, meta = pack_kv(y.reshape(1), route_group, kv, queries)
    k6 = (meta[0] - (z * NY + y)) & (NZ * NY - 1)
    dz = (((y + k6) >> 2) & (NZ - 1)).reshape(1)
    zr1 = lax.all_to_all(zs1, "z", 0, 0, tiled=True)

    tile, queries = lax.optimization_barrier((tile, queries))
    qy = pack_q(tile, queries.reshape(ROWS, QA + QB, UNIT, HD))
    n = NZ * PER
    qy = [qy[:n]] + [side(qy[k * n:(k + 1) * n], k) for k in range(1, NY)]
    zs2, zs3 = assemble(qy)
    zs2, zs3, note1, note2, dz = lax.optimization_barrier((zs2, zs3, note1, note2, dz))
    zr2 = lax.all_to_all(hop(dz, zs2, zr1), "z", 0, 0, tiled=True)

    run = PER * KV
    part = [zr1[:, k * run:(k + 1) * run].reshape(NZ * PER, KV, UNIT, HD) for k in range(NY)]
    own = unpack_kv(idx1, [part[0]] + [side(part[k], k) for k in range(1, NY)])
    own2 = up(own, 2)
    own1a = lax.ppermute(own, "seq", [(i, i + 1) for i in range(0, NS, 2)])
    own1b = lax.ppermute(own2, "seq", [(i + 1, i) for i in range(0, NS, 2)])
    zs3, own2, own1a, own1b = lax.optimization_barrier((zs3, own2, own1a, own1b))
    zr3 = lax.all_to_all(zs3, "z", 0, 0, tiled=True)

    came = zr2[:EXT // HOP, SLOT2 - HOP:].reshape(EXT, UNIT, HD)
    came = jnp.where((k6 & 1) != 0, side(came, 1), came)
    came = jnp.where((k6 & 2) != 0, side(came, 2), came)
    ext = came.reshape(3, EXT // 3, UNIT, HD)
    ext0 = ext[:, :KV]
    rows, segk = window(
        s.reshape(1), (note2, note1, note), (own2, own1a, own1b, own), (up(ext0, 2), up(ext0, 1), ext0)
    )
    kvt, segq = rows.transpose(1, 0, 2), segment_ids.reshape(ROWS, 1)
    out, done = attend(0, unpack_q(KV, QA, idx2, note, zr2, ext), kvt, segq, segk)
    return attend(1, unpack_q(KV + QA, QB, idx3, note, zr3, ext, done), kvt, segq, segk, out)


def solution(mesh):
    fine = Mesh(mesh.devices.reshape(NZ, NY, NS), ("z", "y", "seq"))
    rows = ("z", "y", "seq")
    return jax.shard_map(
        on_device,
        mesh=fine,
        in_specs=(
            P(rows, None),
            P(rows, None, None, None),
            P(rows),
            P(rows),
            P(("z", "y"), "seq"),
        ),
        out_specs=P(rows, None),
        check_vma=False,
    )
```
